128 devices in a mesh: dapw: 32 (over y, z_hi, x), dapn: 4 (over z_lo, core).
Axes of the slice: x: 4, y: 4, z: 4 (z_hi: 2, z_lo: 2; z = z_hi * 2 + z_lo), core: 2. Of those that a mesh axis runs over, the one named last changes fastest.
Arguments:
- homolog_embedding: bfloat16 [2048, 512, 256], P(('dapw', 'dapn')), may hold values from -6 to 6
- alignment_mask: int32 [2048, 512], P(('dapw', 'dapn')), may hold values 0 or 1
- pairwise_features: bfloat16 [128, 512, 512], P('dapn', 'dapw'), may hold values from -3 to 3
- residue_validity_mask: int32 [512], replicated, may hold values 0 or 1
- left_right_coefficients: bfloat16 [256, 64], replicated, may hold values from -0.375 to 0.375
- outer_output_weight: bfloat16 [1024, 128], replicated, may hold values from -1 to 1
- triangle_input_weight: bfloat16 [4, 128, 128], P(None, None, 'dapn'), may hold values from -0.5 to 0.5
- triangle_gate_weight: bfloat16 [128, 128], P(None, 'dapn'), may hold values from -0.5 to 0.5
- triangle_output_weight: bfloat16 [128, 128], replicated, may hold values from -0.5 to 0.5
Outputs:
- pair_out: bfloat16 [128, 512, 512], P('dapn', 'dapw')
The draws below stay inside these ranges and needn't reach their ends.
All inputs are finite; a program needn't handle non-finite values. No bound on the sum of `alignment_mask` on one device may be relied on, other than what follows from the above.
Results may differ from the reference program's by a relative error of at most 0.015.
Values may be sent and summed in bfloat16 or wider, within the bound.
A program may use at most 320 MiB of HBM per device.

```python
import jax
import jax.numpy as jnp
from jax import lax

MULTI_DEPTH = 256
C_Z = 128
LATENT_WIDTH = 32
RES_W = 16
HOMOLOG_NUMBER = 2048
AMINO_NUMBER = 512
N_DAPW = 32


def with_ends(values, rng, smallest, top_value):
    longest = values.shape.index(max(values.shape))
    spots = []
    for shift in (0, 1):
        where = [jax.random.randint(jax.random.fold_in(rng, axis), (), 0, length) for axis, length in enumerate(values.shape)]
        where[longest] = (where[longest] + shift) % values.shape[longest]
        spots.append(tuple(where))
    return values.at[spots[0]].set(smallest).at[spots[1]].set(top_value)


def block_levels(stream_key, extent, split, least, top_value):
    factor_of, own = 1.0, jax.random.fold_in(stream_key, 6)
    for dim, shards_of in split:
        heights = jnp.exp(jax.random.uniform(jax.random.fold_in(own, dim), (shards_of,), jnp.float32, least / len(split), top_value / len(split)))
        factor_of = factor_of * jnp.repeat(heights, extent[dim] // shards_of).reshape([-1 if axis == dim else 1 for axis in range(len(extent))])
    return factor_of


def bell_draw(key, dims, scale, limit, shards=(), kind=jnp.bfloat16):
    entries = scale * jax.random.normal(key, dims, jnp.float32)
    if shards:
        entries = entries * block_levels(key, dims, shards, -0.22, 0.18)
    return jnp.clip(entries, -limit, limit).astype(kind)


def setup_inputs(seed: int = 0) -> dict:
    arg_keys = jax.random.split(jax.random.key(seed), 10)
    return {
        "homolog_embedding": bell_draw(arg_keys[0], (HOMOLOG_NUMBER, AMINO_NUMBER, MULTI_DEPTH), 1.0, 6.0, ((0, 128),)),
        "alignment_mask": with_ends((jax.random.randint(arg_keys[1], (HOMOLOG_NUMBER, AMINO_NUMBER), 0, 8) < 7).astype(jnp.int32), jax.random.fold_in(arg_keys[1], 1), 0, 1),
        "pairwise_features": bell_draw(arg_keys[2], (C_Z, AMINO_NUMBER, AMINO_NUMBER), 0.5, 3.0, ((0, 4), (1, 32))),
        "residue_validity_mask": with_ends((jax.random.randint(arg_keys[3], (AMINO_NUMBER,), 0, 8) < 7).astype(jnp.int32), jax.random.fold_in(arg_keys[3], 1), 0, 1),
        "left_right_coefficients": bell_draw(arg_keys[4], (MULTI_DEPTH, 2 * LATENT_WIDTH), MULTI_DEPTH ** -0.5, 0.375),
        "outer_output_weight": bell_draw(arg_keys[5], (LATENT_WIDTH * LATENT_WIDTH, C_Z), LATENT_WIDTH ** -0.5, 1.0),
        "triangle_input_weight": bell_draw(arg_keys[6], (4, C_Z, C_Z), C_Z ** -0.5, 0.5, ((2, 4),)),
        "triangle_gate_weight": bell_draw(arg_keys[7], (C_Z, C_Z), C_Z ** -0.5, 0.5, ((1, 4),)),
        "triangle_output_weight": bell_draw(arg_keys[8], (C_Z, C_Z), C_Z ** -0.5, 0.5),
    }


def normalize_layer(values, axis):
    center = lax.optimization_barrier(jnp.mean(values, axis, keepdims=True))
    spread = lax.optimization_barrier(jnp.mean(values * values, axis, keepdims=True)) - center * center
    return (values - center) * lax.rsqrt(spread + 1e-05)

def reference(homolog_embedding, alignment_mask, pairwise_features, residue_validity_mask, left_right_coefficients, outer_output_weight, triangle_input_weight, triangle_gate_weight, triangle_output_weight):
    homolog_standardized = normalize_layer(homolog_embedding.astype(jnp.float32), 2).astype(jnp.bfloat16)
    mapped_embedding = jnp.dot(homolog_standardized.reshape(HOMOLOG_NUMBER * AMINO_NUMBER, MULTI_DEPTH), left_right_coefficients, preferred_element_type=jnp.float32).reshape(HOMOLOG_NUMBER, AMINO_NUMBER, 2 * LATENT_WIDTH)
    mapped_embedding = (mapped_embedding * alignment_mask[:, :, None].astype(jnp.float32)).astype(jnp.bfloat16)
    left_cols = mapped_embedding[:, :, :LATENT_WIDTH].reshape(HOMOLOG_NUMBER, AMINO_NUMBER * LATENT_WIDTH)
    right_cols = mapped_embedding[:, :, LATENT_WIDTH:].reshape(HOMOLOG_NUMBER, AMINO_NUMBER * LATENT_WIDTH)
    out_weight = outer_output_weight.astype(jnp.float32).reshape(LATENT_WIDTH, LATENT_WIDTH, C_Z)

    def row_block(index):
        chosen = lax.dynamic_slice_in_dim(left_cols, (index * RES_W * LATENT_WIDTH).astype(jnp.int32), RES_W * LATENT_WIDTH, 1)
        outer_sum = jnp.dot(chosen.T, right_cols, preferred_element_type=jnp.float32) * (1.0 / HOMOLOG_NUMBER)
        outer_sum = outer_sum.reshape(RES_W, LATENT_WIDTH, AMINO_NUMBER, LATENT_WIDTH)
        return jnp.einsum('icjd,cde->eij', outer_sum, out_weight, precision=lax.Precision.HIGHEST)
    blocks = lax.map(row_block, jnp.arange(N_DAPW, dtype=jnp.int32))
    outer_mean = jnp.transpose(blocks, (1, 0, 2, 3)).reshape(C_Z, AMINO_NUMBER, AMINO_NUMBER)
    updated = (pairwise_features.astype(jnp.float32) + outer_mean).astype(jnp.bfloat16)
    normed_pair = normalize_layer(updated.astype(jnp.float32), 0).astype(jnp.bfloat16)
    residue_on = residue_validity_mask.astype(jnp.float32)
    pair_on = residue_on[:, None] * residue_on[None, :]
    normed_wide = normed_pair.astype(jnp.float32)
    proj_wide = triangle_input_weight.astype(jnp.float32)

    def project(index):
        return jnp.einsum('cd,cik->dik', proj_wide[index], normed_wide)
    left_edge = (jax.nn.sigmoid(project(0)) * project(1) * pair_on).astype(jnp.bfloat16)
    right_edge = (jax.nn.sigmoid(project(2)) * project(3) * pair_on).astype(jnp.bfloat16)
    triangle = jnp.einsum('cik,cjk->cij', left_edge.astype(jnp.float32), right_edge.astype(jnp.float32))
    triangle_normed = normalize_layer(triangle, 0).astype(jnp.bfloat16)
    result = jnp.einsum('ce,cij->eij', triangle_output_weight.astype(jnp.float32), triangle_normed.astype(jnp.float32))
    gating = jax.nn.sigmoid(jnp.einsum('ce,cij->eij', triangle_gate_weight.astype(jnp.float32), normed_wide))
    return (updated.astype(jnp.float32) + gating * result).astype(jnp.bfloat16)
```

```python
import jax
import jax.numpy as jnp
from jax import lax
from jax.experimental import pallas as pl
from jax.experimental.pallas import tpu as pltpu
from jax.sharding import PartitionSpec as P

MESH = pl.DeviceIdType.MESH
BF16, F32 = jnp.bfloat16, jnp.float32
EPS = 1e-05
SEQS = 2048
RES = 512
C_Z = 128
LAT = 32
ROWS = 16
QUADS = 4


def position():
    w, n = lax.axis_index("dapw"), lax.axis_index("dapn")
    y, zh, x = w // 8, (w // 4) % 2, w % 4
    return y, zh * 2 + n // 2, x, n % 2


def at(y, z, x, k):
    return y * 8 + (z // 2) * 4 + x, (z % 2) * 2 + k


def remote(src, dst, send, recv, device):
    return pltpu.make_async_remote_copy(
        src_ref=src, dst_ref=dst, send_sem=send, recv_sem=recv, device_id=device, device_id_type=MESH
    )


def arrived(ref, sem):
    pltpu.make_async_copy(ref, ref, sem).wait()


def signal(sem, device):
    pl.semaphore_signal(sem, inc=1, device_id=device, device_id_type=MESH)


def lanes(start, size):
    return pl.ds(pl.multiple_of(start, size), size)


def outer_kernel(
    left, right, feat, wq, w2, updated, wfull_out,
    lbuf, rbuf, lt, prod, z_opp, z_up, z_dn, in_a, in_b, in_p, in_m, own, fbuf, fwide, wfull,
    s_f, r_f, s_w, r_w, s_l1, r_l1, s_r1, r_r1, s_l2, r_l2, s_r2, r_r2, s_c, r_c, s_z, r_z,
):
    y, z, x, k = position()
    zh, zl = z // 2, z % 2
    w, n = at(y, z, x, k)
    yk = y * 2 + k
    ya, yb, yo = (y + 1) % 4, (y + 3) % 4, (y + 2) % 4
    xa, xb, xo = (x + 1) % 4, (x + 3) % 4, (x + 2) % 4
    za, zb = (z + 1) % 4, (z + 3) % 4
    row_block = y * 8 + k * 4 + z
    same = jnp.where((z == x) & (k == zh), 1, 0)

    barrier = pltpu.get_barrier_semaphore()
    for t in range(1, 8):
        o = (yk + t) % 8
        signal(barrier, at(o // 2, z, x, o % 2))
    for t in range(1, 4):
        signal(barrier, at(y, z, (x + t) % 4, k))
        signal(barrier, (w, (n + t) % 4))
    signal(barrier, at(y, za, x, k))
    signal(barrier, at(y, zb, x, k))
    for t in range(4):
        tw, tn = at(y, x, t, zh)

        @pl.when((tw != w) | (tn != n))
        def _():
            signal(barrier, (tw, tn))

        @pl.when((row_block != w) | (t != n))
        def _():
            signal(barrier, (row_block, jnp.int32(t)))

    pl.semaphore_wait(barrier, 7 + 3 + 3 + 2 + 8 - 2 * same)

    sends = []

    def push(src, dst, send, recv, device):
        copy = remote(src, dst, send, recv, device)
        copy.start()
        sends.append(copy)

    for t in range(1, 8):
        o = (yk + t) % 8
        push(left.at[:, lanes(o * 2048, 2048)], lbuf.at[x, yk], s_l1.at[t], r_l1, at(o // 2, z, x, o % 2))
    pltpu.make_async_copy(left.at[:, lanes(yk * 2048, 2048)], lbuf.at[x, yk], r_l1).start()
    for t in range(1, 4):
        o = (x + t) % 4
        push(right.at[:, :, lanes(o * 128, 128)], rbuf.at[:, x, yk], s_r1.at[t], r_r1, at(y, z, o, k))
    pltpu.make_async_copy(right.at[:, :, lanes(x * 128, 128)], rbuf.at[:, x, yk], r_r1).start()

    def feature_copy(t):
        tw, tn = at(y, x, t, zh)
        return tw, tn, remote(
            feat.at[:, :, t * 128 : (t + 1) * 128], fbuf.at[pl.ds(n * 32, 32)], s_f.at[t], r_f, (tw, tn)
        )

    for t in range(4):
        tw, tn, copy = feature_copy(t)

        @pl.when((tw != w) | (tn != n))
        def _():
            copy.start()

        @pl.when((tw == w) & (tn == n))
        def _():
            pltpu.make_async_copy(feat.at[:, :, t * 128 : (t + 1) * 128], fbuf.at[pl.ds(n * 32, 32)], r_f).start()

    for t in range(1, 4):
        push(wq, wfull.at[n], s_w.at[t], r_w, (w, (n + t) % 4))
    pltpu.make_async_copy(wq, wfull.at[n], r_w).start()

    def left_part(slab, j):
        group = (z + (2, 0, 1, 3)[j]) % 4
        return lbuf.at[slab, :, :, lanes(group * 512, 512)]

    def right_part(yy, kk, q):
        return rbuf.at[q * 8 : (q + 1) * 8, :, yy * 2 + kk]

    arrived(lbuf.at[x], r_l1)
    for j in range(QUADS):
        push(left_part(x, j), left_part(x, j), s_l2.at[0, j], r_l2.at[0, j], at(y, z, xa, k))
        push(left_part(x, j), left_part(x, j), s_l2.at[1, j], r_l2.at[1, j], at(y, z, xb, k))
    arrived(rbuf.at[:, :, yk], r_r1)
    for q in range(QUADS):
        mine = right_part(y, k, q)
        push(mine, mine, s_r2.at[0, q], r_r2.at[0, q], at(ya, z, x, k))
        push(mine, mine, s_r2.at[1, q], r_r2.at[1, q], at(yb, z, x, k))
        push(mine, mine, s_c.at[0, q], r_c.at[0, q], at(y, z, x, 1 - k))

    def product(a, q):
        def step(p, carry):
            d = q * 8 + p * 2
            pair = jnp.concatenate(
                [rbuf[d].reshape(512, 128), rbuf[d + 1].reshape(512, 128)], axis=1
            )
            value = jnp.dot(lt[a], pair, preferred_element_type=F32).astype(BF16)
            for h in range(2):
                prod[pl.ds(a * 16, 16), pl.ds(pl.multiple_of((d + h) * 32, 32), 32), :] = value[
                    :, h * 128 : (h + 1) * 128
                ].reshape(16, 32, 128)
            return carry

        lax.fori_loop(0, 4, step, 0)

    def means(a, store):
        def step(p, carry):
            i = p * 2
            pair = jnp.concatenate([prod[a * 16 + i], prod[a * 16 + i + 1]], axis=1)
            value = jnp.dot(w2[...], pair, preferred_element_type=F32) * (1.0 / SEQS)
            store(i, value[:, :128])
            store(i + 1, value[:, 128:])
            return carry

        return step

    for step in range(QUADS + 2):
        if step < QUADS:
            j = q = step
            arrived(left_part(xb, j), r_l2.at[0, j])
            if j % 2 == 0:
                push(left_part(xb, j), left_part(xb, j), s_l2.at[2, j], r_l2.at[2, j], at(y, z, xa, k))
            arrived(left_part(xa, j), r_l2.at[1, j])
            if j % 2 == 1:
                push(left_part(xa, j), left_part(xa, j), s_l2.at[2, j], r_l2.at[2, j], at(y, z, xb, k))
            for src, up in ((yb, True), (ya, False)):
                part = right_part(src, k, q)
                arrived(part, r_r2.at[0 if up else 1, q])
                if up == (q % 2 == 0):
                    push(part, part, s_r2.at[2, q], r_r2.at[2, q], at(ya if up else yb, z, x, k))
                side = 1 if up else 2
                push(part, part, s_c.at[side, q], r_c.at[side, q], at(y, z, x, 1 - k))
        if 0 <= step - 1 < QUADS:
            j = q = step - 1
            part = right_part(yo, k, q)
            arrived(part, r_r2.at[2, q])
            push(part, part, s_c.at[3, q], r_c.at[3, q], at(y, z, x, 1 - k))
            arrived(left_part(xo, j), r_l2.at[2, j])
            group = (z + (2, 0, 1, 3)[j]) % 4
            lt[j] = lbuf[:, :, :, lanes(group * 512, 512)].reshape(512, 512).T
        if 0 <= step - 2:
            q = step - 2
            for side, src in ((0, y), (1, yb), (2, ya), (3, yo)):
                arrived(right_part(src, 1 - k, q), r_c.at[side, q])
            if q < QUADS - 1:
                lax.fori_loop(0, q + 1, lambda a, c: (product(a, q), c)[1], 0)
                if q > 0:
                    lax.fori_loop(0, q, lambda b, c: (product(q, b), c)[1], 0)
                continue
            up, down = at(y, za, x, k), at(y, zb, x, k)
            product(0, q)

            def store_opp(i, value):
                z_opp[i] = value.astype(BF16)

            lax.fori_loop(0, 4, means(0, store_opp), 0)
            push(z_opp.at[0:8], in_a, s_z.at[0], r_z.at[0], up)
            lax.fori_loop(4, 8, means(0, store_opp), 0)
            push(z_opp.at[8:16], in_b, s_z.at[1], r_z.at[1], down)

            def store_own(i, value):
                own[i] = value

            product(1, q)
            lax.fori_loop(0, 8, means(1, store_own), 0)

            def store_up(i, value):
                z_up[i] = value.astype(BF16)

            def store_up_sum(i, value):
                z_up[i] = (value + in_a[i].astype(F32)).astype(BF16)

            product(2, q)
            arrived(in_a, r_z.at[0])
            lax.fori_loop(0, 4, means(2, store_up_sum), 0)
            push(z_up.at[0:8], in_p.at[0:8], s_z.at[2], r_z.at[2], up)
            lax.fori_loop(4, 8, means(2, store_up), 0)
            push(z_up.at[8:16], in_p.at[8:16], s_z.at[3], r_z.at[3], up)

            def store_down(i, value):
                z_dn[i] = value.astype(BF16)

            def store_down_sum(i, value):
                z_dn[i] = (value + in_b[i - 8].astype(F32)).astype(BF16)

            product(3, q)
            lax.fori_loop(0, 3, lambda b, c: (product(3, b), c)[1], 0)
            arrived(in_b, r_z.at[1])
            lax.fori_loop(4, 8, means(3, store_down_sum), 0)
            push(z_dn.at[8:16], in_m.at[8:16], s_z.at[4], r_z.at[4], down)
            lax.fori_loop(0, 4, means(3, store_down), 0)
            push(z_dn.at[0:8], in_m.at[0:8], s_z.at[5], r_z.at[5], down)

    arrived(fbuf, r_f)
    fwide[...] = fbuf[...].astype(F32)
    arrived(wfull, r_w)
    wfull_out[...] = wfull[...]
    arrived(in_p.at[0:8], r_z.at[2])
    arrived(in_p.at[8:16], r_z.at[3])
    arrived(in_m.at[8:16], r_z.at[4])
    arrived(in_m.at[0:8], r_z.at[5])
    for i in range(ROWS):
        total = own[i] + in_p[i].astype(F32) + in_m[i].astype(F32)
        updated[i] = (fwide[:, i, :] + total).astype(BF16)

    for copy in sends:
        copy.wait_send()
    for t in range(4):
        tw, tn, copy = feature_copy(t)

        @pl.when((tw != w) | (tn != n))
        def _():
            copy.wait_send()


def triangle_kernel(
    updated, wfull, wout, mrow, mcol, out,
    wide, gate, outgoing, edges, tri, back, tile, landed,
    s_e, r_e, s_t, r_t, s_o, r_o,
):
    y, z, x, k = position()
    w, n = at(y, z, x, k)
    me = w * 4 + n
    row_block = y * 8 + k * 4 + z

    barrier = pltpu.get_barrier_semaphore()

    def greet(t, carry):
        o = (me + t) % 128
        signal(barrier, (o // 4, o % 4))
        return carry

    lax.fori_loop(1, 128, greet, 0)

    weights = wfull[...].reshape(640, C_Z)
    col_on = mcol[pl.ds(x, 1), :]
    for i in range(ROWS):
        u = updated[i].astype(F32)
        center = jnp.sum(u, 0, keepdims=True) * (1.0 / C_Z)
        spread = jnp.sum(u * u, 0, keepdims=True) * (1.0 / C_Z) - center * center
        normed = ((u - center) * lax.rsqrt(spread + EPS)).astype(BF16)
        proj = jnp.dot(weights, normed, preferred_element_type=F32)
        on = col_on * mrow[row_block * ROWS + i].astype(F32)
        for c in range(4):
            base = c * 160
            wide[0, c * 32 : (c + 1) * 32, i, :] = (
                jax.nn.sigmoid(proj[base : base + 32]) * proj[base + 32 : base + 64] * on
            )
            wide[1, c * 32 : (c + 1) * 32, i, :] = (
                jax.nn.sigmoid(proj[base + 64 : base + 96]) * proj[base + 96 : base + 128] * on
            )
            gate[i, c * 32 : (c + 1) * 32, :] = proj[base + 128 : base + 160]
    for h in range(2):
        outgoing[:, h] = wide[h].astype(BF16)

    pl.semaphore_wait(barrier, 127)

    def send_edges(t, carry):
        o = (me + t) % 128
        remote(outgoing.at[o], edges.at[:, x, row_block], s_e, r_e, (o // 4, o % 4)).start()
        return carry

    pltpu.make_async_copy(outgoing.at[me], edges.at[:, x, row_block], r_e).start()
    lax.fori_loop(1, 128, send_edges, 0)
    gate[...] = jax.nn.sigmoid(gate[...])
    arrived(edges, r_e)

    first = jnp.concatenate([edges[0, b].reshape(RES, 128) for b in range(4)], axis=1)
    for b in range(4):
        second = jnp.concatenate(
            [edges[1, c, b * 8 : (b + 1) * 8].reshape(128, 128) for c in range(4)], axis=1
        )
        value = lax.dot_general(first, second, (((1,), (1,)), ((), ())), preferred_element_type=F32)
        tri[b] = value.astype(BF16).reshape(32, ROWS, 128)

        def send_back(t, carry):
            r = (row_block + t) % 32
            tw, tn = at(r // 8, r % 4, jnp.int32(b), (r // 4) % 2)

            @pl.when((tw != w) | (tn != n))
            def _():
                remote(tri.at[b, r], back.at[me], s_t, r_t, (tw, tn)).start()

            @pl.when((tw == w) & (tn == n))
            def _():
                pltpu.make_async_copy(tri.at[b, r], back.at[me], r_t).start()

            return carry

        lax.fori_loop(0, 32, send_back, 0)

    arrived(back, r_t)
    wide[0] = back[...].astype(F32)
    for i in range(ROWS):
        t = wide[0, :, i, :]
        center = jnp.sum(t, 0, keepdims=True) * (1.0 / C_Z)
        spread = jnp.sum(t * t, 0, keepdims=True) * (1.0 / C_Z) - center * center
        normed = ((t - center) * lax.rsqrt(spread + EPS)).astype(BF16)
        result = jnp.dot(wout[...], normed, preferred_element_type=F32)
        wide[1, :, i, :] = updated[i].astype(F32) + gate[i] * result
    tile[...] = wide[1].astype(BF16)

    def out_copy(q):
        return remote(
            tile.at[q * 32 : (q + 1) * 32],
            landed.at[:, :, lanes(x * 128, 128)],
            s_o.at[q], r_o, (row_block, jnp.int32(q)),
        )

    for q in range(4):
        away = (row_block != w) | (n != q)

        @pl.when(away)
        def _():
            out_copy(q).start()

        @pl.when(jnp.logical_not(away))
        def _():
            pltpu.make_async_copy(
                tile.at[q * 32 : (q + 1) * 32], landed.at[:, :, lanes(x * 128, 128)], r_o
            ).start()

    arrived(landed, r_o)
    out[...] = landed[...]

    arrived(outgoing.at[0:127], s_e)
    arrived(back.at[0:127], s_t)
    for q in range(4):

        @pl.when((row_block != w) | (n != q))
        def _():
            out_copy(q).wait_send()


def vmem(count):
    return [pl.BlockSpec(memory_space=pltpu.VMEM)] * count


def outer_call(left, right, feat, wq, w2):
    dma = pltpu.SemaphoreType.DMA
    return pl.pallas_call(
        outer_kernel,
        name="outer",
        out_shape=(
            jax.ShapeDtypeStruct((ROWS, C_Z, 128), BF16),
            jax.ShapeDtypeStruct((4, 160, C_Z), BF16),
        ),
        in_specs=vmem(5),
        out_specs=tuple(vmem(2)),
        scratch_shapes=[
            pltpu.VMEM((4, 8, 16, 2048), BF16),
            pltpu.VMEM((LAT, 4, 8, 16, 128), BF16),
            pltpu.VMEM((4, 512, 512), BF16),
            pltpu.VMEM((64, LAT * LAT, 128), BF16),
            pltpu.VMEM((ROWS, C_Z, 128), BF16),
            pltpu.VMEM((ROWS, C_Z, 128), BF16),
            pltpu.VMEM((ROWS, C_Z, 128), BF16),
            pltpu.VMEM((8, C_Z, 128), BF16),
            pltpu.VMEM((8, C_Z, 128), BF16),
            pltpu.VMEM((ROWS, C_Z, 128), BF16),
            pltpu.VMEM((ROWS, C_Z, 128), BF16),
            pltpu.VMEM((ROWS, C_Z, 128), F32),
            pltpu.VMEM((C_Z, ROWS, 128), BF16),
            pltpu.VMEM((C_Z, ROWS, 128), F32),
            pltpu.VMEM((4, 160, C_Z), BF16),
            dma((4,)), dma, dma((4,)), dma,
            dma((8,)), dma, dma((4,)), dma,
            dma((3, 4)), dma((3, 4)), dma((3, 4)), dma((3, 4)),
            dma((4, 4)), dma((4, 4)), dma((6,)), dma((6,)),
        ],
        compiler_params=pltpu.CompilerParams(
            collective_id=0, has_side_effects=True, vmem_limit_bytes=48 * 2**20
        ),
        cost_estimate=pl.CostEstimate(flops=11 * 10**9, bytes_accessed=3 * 2**20, transcendentals=0),
    )(left, right, feat, wq, w2)


def triangle_call(updated, wfull, wout, mrow, mcol):
    dma = pltpu.SemaphoreType.DMA
    return pl.pallas_call(
        triangle_kernel,
        name="triangle",
        out_shape=jax.ShapeDtypeStruct((32, ROWS, RES), BF16),
        in_specs=vmem(3) + [pl.BlockSpec(memory_space=pltpu.SMEM)] + vmem(1),
        out_specs=pl.BlockSpec(memory_space=pltpu.VMEM),
        scratch_shapes=[
            pltpu.VMEM((2, C_Z, ROWS, 128), F32),
            pltpu.VMEM((ROWS, C_Z, 128), F32),
            pltpu.VMEM((C_Z, 2, ROWS, 128), BF16),
            pltpu.VMEM((2, 4, 32, ROWS, 128), BF16),
            pltpu.VMEM((4, 32, ROWS, 128), BF16),
            pltpu.VMEM((C_Z, ROWS, 128), BF16),
            pltpu.VMEM((C_Z, ROWS, 128), BF16),
            pltpu.VMEM((32, ROWS, RES), BF16),
            dma, dma, dma, dma, dma((4,)), dma,
        ],
        compiler_params=pltpu.CompilerParams(
            collective_id=1, has_side_effects=True, vmem_limit_bytes=40 * 2**20
        ),
        cost_estimate=pl.CostEstimate(flops=10**9, bytes_accessed=2 * 2**20, transcendentals=10**6),
    )(updated, wfull, wout, mrow, mcol)


def body(
    homolog_embedding,
    alignment_mask,
    pairwise_features,
    residue_validity_mask,
    left_right_coefficients,
    outer_output_weight,
    triangle_input_weight,
    triangle_gate_weight,
    triangle_output_weight,
):
    seqs, residues, features = homolog_embedding.shape
    msa = homolog_embedding.astype(F32)
    center = jnp.mean(msa, 2, keepdims=True)
    spread = jnp.mean(msa * msa, 2, keepdims=True) - center * center
    normed = ((msa - center) * lax.rsqrt(spread + EPS)).astype(BF16)
    edges = jnp.dot(
        normed.reshape(seqs * residues, features),
        left_right_coefficients,
        preferred_element_type=F32,
    )
    edges = edges.reshape(seqs, residues, 2 * LAT) * alignment_mask[:, :, None].astype(F32)
    edges = edges.astype(BF16)
    left = edges[:, :, :LAT].reshape(seqs, residues * LAT)
    right = jnp.transpose(edges[:, :, LAT:], (2, 0, 1))

    w2 = jnp.transpose(outer_output_weight.reshape(LAT, LAT, C_Z), (2, 1, 0)).reshape(C_Z, LAT * LAT)
    wq = jnp.concatenate([triangle_input_weight, triangle_gate_weight[None]], 0)
    wq = jnp.transpose(wq, (0, 2, 1)).reshape(160, C_Z)
    updated, wfull = outer_call(left, right, pairwise_features, wq, w2)
    return triangle_call(
        updated, wfull, triangle_output_weight.T,
        residue_validity_mask, residue_validity_mask.astype(F32).reshape(4, 128),
    )


def solution(mesh):
    return jax.shard_map(
        body,
        mesh=mesh,
        in_specs=(
            P(("dapw", "dapn"), None, None),
            P(("dapw", "dapn"), None),
            P("dapn", "dapw", None),
            P(),
            P(),
            P(),
            P(None, None, "dapn"),
            P(None, "dapn"),
            P(),
        ),
        out_specs=P("dapn", "dapw", None),
        check_vma=False,
    )
```

```python
import jax
import jax.numpy as jnp
from jax import lax
from jax.experimental import pallas as pl
from jax.experimental.pallas import tpu as pltpu
from jax.sharding import PartitionSpec as P

MESH = pl.DeviceIdType.MESH
BF16, F32 = jnp.bfloat16, jnp.float32
EPS = 1e-05
SEQS = 2048
RES = 512
C_Z = 128
LAT = 32
ROWS = 16
QUADS = 4


def position():
    w, n = lax.axis_index("dapw"), lax.axis_index("dapn")
    y, zh, x = w // 8, (w // 4) % 2, w % 4
    return y, zh * 2 + n // 2, x, n % 2


def at(y, z, x, k):
    return y * 8 + (z // 2) * 4 + x, (z % 2) * 2 + k


def block_of(y, z, k):
    return y * 8 + (z // 2) * 4 + k * 2 + z % 2


def remote(src, dst, send, recv, device):
    return pltpu.make_async_remote_copy(
        src_ref=src, dst_ref=dst, send_sem=send, recv_sem=recv, device_id=device, device_id_type=MESH
    )


def arrived(ref, sem):
    pltpu.make_async_copy(ref, ref, sem).wait()


def signal(sem, device):
    pl.semaphore_signal(sem, inc=1, device_id=device, device_id_type=MESH)


def lanes(start, size):
    return pl.ds(pl.multiple_of(start, size), size)


def kernel(
    msa, msa_mask, feat, coef, w2, wq, wout, mrow, mcol, out,
    held, lwide, rwide, left, right, lbuf, rbuf, lt, prod,
    z_opp, z_up, z_dn, in_a, in_b, in_p, in_m, own, fbuf, wide, wfull,
    updated, gate, outgoing, edges, tri, back, tile, landed,
    s_x, s_f, r_f, s_w, r_w, s_l1, r_l1, s_r1, r_r1, s_l2, r_l2, s_r2, r_r2, s_c, r_c, s_z, r_z,
    s_e, r_e, s_t, r_t, s_o, r_o,
):
    y, z, x, k = position()
    feature_z, feature_k = (z // 2) * 2 + x % 2, x // 2
    w, n = at(y, z, x, k)
    me = w * 4 + n
    yk = y * 2 + k
    ya, yb, yo = (y + 1) % 4, (y + 3) % 4, (y + 2) % 4
    xa, xb, xo = (x + 1) % 4, (x + 3) % 4, (x + 2) % 4
    za, zb, zo = (z + 1) % 4, (z + 3) % 4, (z + 2) % 4
    up, down = at(y, za, x, k), at(y, zb, x, k)
    row_block = block_of(y, z, k)

    def load(g):
        part = pl.ds(g * 4, 4)
        return pltpu.make_async_copy(msa.at[part], held.at[part], s_x.at[g])

    for g in range(4):
        load(g).start()

    barrier = pltpu.get_barrier_semaphore()

    def greet(t, carry):
        o = (me + t) % 128
        signal(barrier, (o // 4, o % 4))
        return carry

    lax.fori_loop(1, 128, greet, 0)

    wl, wr = coef[:, :LAT], coef[:, LAT:]
    wide_coef = jnp.concatenate([wl] * 4 + [wr] * 4, axis=1)
    column_sum = jnp.sum(wide_coef.astype(F32), 0, keepdims=True)
    mask_columns = msa_mask[...].astype(F32).T
    lane_part = lax.broadcasted_iota(jnp.int32, (1, 128), 1) // LAT
    for g in range(4):
        load(g).wait()
        packed = jnp.zeros((RES, 128), F32)
        for h in range(4):
            s = g * 4 + h
            values = held[s]
            v = values.astype(F32)
            center = jnp.sum(v, 1, keepdims=True) * (1.0 / 256)
            spread = jnp.sum(v * v, 1, keepdims=True) * (1.0 / 256) - center * center
            scale = lax.rsqrt(spread + EPS) * mask_columns[:, s : s + 1]
            mapped = jnp.dot(values, wide_coef, preferred_element_type=F32)
            mapped = (mapped - center * column_sum) * scale
            lefts = mapped[:, :128].reshape(16, 4, 8, 128)
            merged = lefts[:, 0]
            for rr in range(1, 4):
                merged = jnp.where(lane_part[None] == rr, lefts[:, rr], merged)
            lwide[s] = merged.reshape(128, 128)
            packed = jnp.where(lane_part == h, mapped[:, 128:], packed)
        rwide[g * 4 : (g + 1) * 4] = packed.T.reshape(4, LAT, RES)
    for t in range(128):
        left[:, t * 128 : (t + 1) * 128] = lwide[:, t, :].astype(BF16)
    for d in range(LAT):
        right[d] = rwide[:, d, :].astype(BF16)

    pl.semaphore_wait(barrier, 127)

    sends = []

    def push(src, dst, send, recv, device):
        copy = remote(src, dst, send, recv, device)
        copy.start()
        sends.append(copy)

    def left_block(o, h):
        return left.at[:, lanes((o // 2) * 4096 + h * 2048 + (o % 2) * 1024, 1024)]

    for h in range(2):
        target = lbuf.at[x, yk, :, h * 1024 : (h + 1) * 1024]
        for t in range(1, 8):
            o = (yk + t) % 8
            push(left_block(o, h), target, s_l1.at[h, t], r_l1, at(o // 2, z, x, o % 2))
        pltpu.make_async_copy(left_block(yk, h), target, r_l1).start()
    for t in range(1, 4):
        o = (x + t) % 4
        push(right.at[:, :, lanes(o * 128, 128)], rbuf.at[:, x, yk], s_r1.at[t], r_r1, at(y, z, o, k))
    pltpu.make_async_copy(right.at[:, :, lanes(x * 128, 128)], rbuf.at[:, x, yk], r_r1).start()

    for t in range(1, 4):
        push(wq, wfull.at[n], s_w.at[t], r_w, (w, (n + t) % 4))
    pltpu.make_async_copy(wq, wfull.at[n], r_w).start()

    def feature_copy(t):
        tw, tn = at(y, feature_z, t, feature_k)
        return tw, tn, remote(
            feat.at[:, :, t * 128 : (t + 1) * 128], fbuf.at[pl.ds(n * 32, 32)], s_f.at[t], r_f, (tw, tn)
        )

    def half_of(p):
        return (z // 2 + 1 + p // 2) % 2

    def left_part(slab, p):
        return lbuf.at[slab, (p % 2) * 4 : (p % 2) * 4 + 4, :, lanes(half_of(p) * 1024, 1024)]

    def right_part(yy, kk, q):
        return rbuf.at[q * 8 : (q + 1) * 8, :, yy * 2 + kk]

    arrived(lbuf.at[x], r_l1)
    for p in range(QUADS):
        push(left_part(x, p), left_part(x, p), s_l2.at[0, p], r_l2.at[0, p], at(y, z, xa, k))
        push(left_part(x, p), left_part(x, p), s_l2.at[1, p], r_l2.at[1, p], at(y, z, xb, k))
    arrived(rbuf.at[:, :, yk], r_r1)
    for q in range(QUADS):
        mine = right_part(y, k, q)
        push(mine, mine, s_r2.at[0, q], r_r2.at[0, q], at(ya, z, x, k))
        push(mine, mine, s_r2.at[1, q], r_r2.at[1, q], at(yb, z, x, k))
        push(mine, mine, s_c.at[0, q], r_c.at[0, q], at(y, z, x, 1 - k))

    def product(a, q):
        parts = [rbuf[q * 8 + h].reshape(512, 128) for h in range(8)]
        value = jnp.dot(lt[a], jnp.concatenate(parts, axis=1), preferred_element_type=F32).astype(BF16)
        for h in range(8):
            prod[pl.ds(a * 16, 16), pl.ds(pl.multiple_of((q * 8 + h) * 32, 32), 32), :] = value[
                :, h * 128 : (h + 1) * 128
            ].reshape(16, 32, 128)

    def products(half, first, last):
        def step(t, carry):
            product(half * 2 + t % 2, first + t // 2)
            return carry

        lax.fori_loop(0, (last - first) * 2, step, 0)

    def means(a, part, store):
        rows = [prod[a * 16 + part * 8 + h] for h in range(8)]
        value = jnp.dot(w2[...], jnp.concatenate(rows, axis=1), preferred_element_type=F32) * (1.0 / SEQS)
        for h in range(8):
            store(part * 8 + h, value[:, h * 128 : (h + 1) * 128])

    for step in range(QUADS + 2):
        if step < QUADS:
            p = q = step
            for src, upward in ((yb, True), (ya, False)):
                part = right_part(src, k, q)
                arrived(part, r_r2.at[0 if upward else 1, q])
                if upward == (q % 2 == 0):
                    push(part, part, s_r2.at[2, q], r_r2.at[2, q], at(ya if upward else yb, z, x, k))
                side = 1 if upward else 2
                push(part, part, s_c.at[side, q], r_c.at[side, q], at(y, z, x, 1 - k))
            for src, upward in ((xb, True), (xa, False)):
                part = left_part(src, p)
                arrived(part, r_l2.at[0 if upward else 1, p])
                if upward == (p % 2 == 0):
                    push(part, part, s_l2.at[2, p], r_l2.at[2, p], at(y, z, xa if upward else xb, k))
        if 0 <= step - 1 < QUADS:
            p = q = step - 1
            part = right_part(yo, k, q)
            arrived(part, r_r2.at[2, q])
            push(part, part, s_c.at[3, q], r_c.at[3, q], at(y, z, x, 1 - k))
            arrived(left_part(xo, p), r_l2.at[2, p])
            if p % 2 == 1:
                half = half_of(p)
                turned = lbuf[:, :, :, lanes(half * 1024, 1024)].reshape(512, 1024).T
                for m in range(32):
                    zl, i = m // 16, m % 16
                    row = ((i % 8) * 4 + zl * 2 + i // 8) * 32
                    lt[half * 2 + zl, i * 32 : (i + 1) * 32] = turned[row : row + 32]
        if 0 <= step - 2:
            q = step - 2
            for side, src in ((0, y), (1, yb), (2, ya), (3, yo)):
                arrived(right_part(src, 1 - k, q), r_c.at[side, q])
            if q < QUADS - 1:
                products(half_of(0), q, q + 1)
                if q == QUADS - 2:
                    products(half_of(2), 0, q + 1)

    for t in range(4):
        tw, tn, copy = feature_copy(t)

        @pl.when((tw != w) | (tn != n))
        def _():
            copy.start()

        @pl.when((tw == w) & (tn == n))
        def _():
            pltpu.make_async_copy(feat.at[:, :, t * 128 : (t + 1) * 128], fbuf.at[pl.ds(n * 32, 32)], r_f).start()

    def store_opp(i, value):
        z_opp[i] = value.astype(BF16)

    def store_own(i, value):
        own[i] = value

    def store_up(i, value):
        z_up[i] = value.astype(BF16)

    def store_up_sum(i, value):
        z_up[i] = (value + in_a[i].astype(F32)).astype(BF16)

    def store_down(i, value):
        z_dn[i] = value.astype(BF16)

    def store_down_sum(i, value):
        z_dn[i] = (value + in_b[i - 8].astype(F32)).astype(BF16)

    product(zo, 3)
    means(zo, 0, store_opp)
    push(z_opp.at[0:8], in_a, s_z.at[0], r_z.at[0], up)
    means(zo, 1, store_opp)
    push(z_opp.at[8:16], in_b, s_z.at[1], r_z.at[1], down)
    product(za, 3)
    means(za, 1, store_up)
    push(z_up.at[8:16], in_p.at[8:16], s_z.at[3], r_z.at[3], up)
    product(zb, 3)
    means(zb, 0, store_down)
    push(z_dn.at[0:8], in_m.at[0:8], s_z.at[5], r_z.at[5], down)
    arrived(in_a, r_z.at[0])
    means(za, 0, store_up_sum)
    push(z_up.at[0:8], in_p.at[0:8], s_z.at[2], r_z.at[2], up)
    arrived(in_b, r_z.at[1])
    means(zb, 1, store_down_sum)
    push(z_dn.at[8:16], in_m.at[8:16], s_z.at[4], r_z.at[4], down)
    product(z, 3)
    for part in range(2):
        means(z, part, store_own)

    arrived(fbuf, r_f)
    wide[0] = fbuf[...].astype(F32)
    arrived(wfull, r_w)
    weights = wfull[...].reshape(640, C_Z)
    col_on = mcol[pl.ds(x, 1), :]
    arrived(in_p.at[8:16], r_z.at[3])
    arrived(in_m.at[0:8], r_z.at[5])
    arrived(in_p.at[0:8], r_z.at[2])
    arrived(in_m.at[8:16], r_z.at[4])
    for i in range(ROWS):
        total = own[i] + in_p[i].astype(F32) + in_m[i].astype(F32)
        updated[i] = (wide[0, :, i, :] + total).astype(BF16)
    for i in range(ROWS):
        u = updated[i].astype(F32)
        center = jnp.sum(u, 0, keepdims=True) * (1.0 / C_Z)
        spread = jnp.sum(u * u, 0, keepdims=True) * (1.0 / C_Z) - center * center
        normed = ((u - center) * lax.rsqrt(spread + EPS)).astype(BF16)
        proj = jnp.dot(weights, normed, preferred_element_type=F32)
        on = col_on * mrow[row_block * ROWS + i].astype(F32)
        for c in range(4):
            base = c * 160
            wide[0, c * 32 : (c + 1) * 32, i, :] = (
                jax.nn.sigmoid(proj[base : base + 32]) * proj[base + 32 : base + 64] * on
            )
            wide[1, c * 32 : (c + 1) * 32, i, :] = (
                jax.nn.sigmoid(proj[base + 64 : base + 96]) * proj[base + 96 : base + 128] * on
            )
            gate[i, c * 32 : (c + 1) * 32, :] = proj[base + 128 : base + 160]
    for h in range(2):
        outgoing[:, h] = wide[h].astype(BF16)

    def send_edges(t, carry):
        o = (me + t * 37) % 128
        remote(outgoing.at[o], edges.at[:, x, row_block], s_e, r_e, (o // 4, o % 4)).start()
        return carry

    pltpu.make_async_copy(outgoing.at[me], edges.at[:, x, row_block], r_e).start()
    lax.fori_loop(1, 128, send_edges, 0)
    gate[...] = jax.nn.sigmoid(gate[...])
    arrived(edges, r_e)

    first = jnp.concatenate([edges[0, b].reshape(RES, 128) for b in range(4)], axis=1)
    for q in (1, 3, 2, 0):
        b = (x + q) % 4
        second = jnp.concatenate(
            [edges[1, c, pl.ds(b * 8, 8)].reshape(128, 128) for c in range(4)], axis=1
        )
        value = lax.dot_general(first, second, (((1,), (1,)), ((), ())), preferred_element_type=F32)
        tri[b] = value.astype(BF16).reshape(32, ROWS, 128)

        def send_back(t, carry):
            r = (row_block + t * 11) % 32
            tw, tn = at(r // 8, ((r // 4) % 2) * 2 + r % 2, b, (r // 2) % 2)

            @pl.when((tw != w) | (tn != n))
            def _():
                remote(tri.at[b, r], back.at[me], s_t, r_t, (tw, tn)).start()

            @pl.when((tw == w) & (tn == n))
            def _():
                pltpu.make_async_copy(tri.at[b, r], back.at[me], r_t).start()

            return carry

        lax.fori_loop(0, 32, send_back, 0)

    arrived(back, r_t)
    wide[0] = back[...].astype(F32)
    for i in range(ROWS):
        t = wide[0, :, i, :]
        center = jnp.sum(t, 0, keepdims=True) * (1.0 / C_Z)
        spread = jnp.sum(t * t, 0, keepdims=True) * (1.0 / C_Z) - center * center
        normed = ((t - center) * lax.rsqrt(spread + EPS)).astype(BF16)
        result = jnp.dot(wout[...], normed, preferred_element_type=F32)
        wide[1, :, i, :] = updated[i].astype(F32) + gate[i] * result
    tile[...] = wide[1].astype(BF16)

    def out_parts(t):
        q = (x + t) % 4
        part = tile.at[pl.ds(q * 32, 32)]
        place = landed.at[:, :, lanes(x * 128, 128)]
        away = (row_block != w) | (n != q)
        return away, part, place, remote(part, place, s_o.at[t], r_o, (row_block, q))

    for t in range(4):
        away, part, place, copy = out_parts(t)

        @pl.when(away)
        def _():
            copy.start()

        @pl.when(jnp.logical_not(away))
        def _():
            pltpu.make_async_copy(part, place, r_o).start()

    arrived(landed, r_o)
    out[...] = landed[...]

    arrived(outgoing.at[0:127], s_e)
    arrived(back.at[0:127], s_t)
    for t in range(4):
        away, part, place, copy = out_parts(t)

        @pl.when(away)
        def _():
            copy.wait_send()

    for copy in sends:
        copy.wait_send()
    for t in range(4):
        tw, tn, copy = feature_copy(t)

        @pl.when((tw != w) | (tn != n))
        def _():
            copy.wait_send()


def call(msa, msa_mask, feat, coef, w2, wq, wout, mrow, mcol):
    dma = pltpu.SemaphoreType.DMA
    vmem = pl.BlockSpec(memory_space=pltpu.VMEM)
    pair = pltpu.VMEM((ROWS, C_Z, 128), BF16)
    return pl.pallas_call(
        kernel,
        name="evoformer",
        out_shape=jax.ShapeDtypeStruct((32, ROWS, RES), BF16),
        in_specs=[pl.BlockSpec(memory_space=pl.ANY)]
        + [vmem] * 6
        + [pl.BlockSpec(memory_space=pltpu.SMEM), vmem],
        out_specs=vmem,
        scratch_shapes=[
            pltpu.VMEM((16, RES, 256), BF16),
            pltpu.VMEM((16, 128, 128), F32),
            pltpu.VMEM((16, LAT, RES), F32),
            pltpu.VMEM((16, RES * LAT), BF16),
            pltpu.VMEM((LAT, 16, RES), BF16),
            pltpu.VMEM((4, 8, 16, 2048), BF16),
            pltpu.VMEM((LAT, 4, 8, 16, 128), BF16),
            pltpu.VMEM((4, 512, 512), BF16),
            pltpu.VMEM((64, LAT * LAT, 128), BF16),
            pair, pair, pair,
            pltpu.VMEM((8, C_Z, 128), BF16),
            pltpu.VMEM((8, C_Z, 128), BF16),
            pair, pair,
            pltpu.VMEM((ROWS, C_Z, 128), F32),
            pltpu.VMEM((C_Z, ROWS, 128), BF16),
            pltpu.VMEM((2, C_Z, ROWS, 128), F32),
            pltpu.VMEM((4, 160, C_Z), BF16),
            pair,
            pltpu.VMEM((ROWS, C_Z, 128), F32),
            pltpu.VMEM((C_Z, 2, ROWS, 128), BF16),
            pltpu.VMEM((2, 4, 32, ROWS, 128), BF16),
            pltpu.VMEM((4, 32, ROWS, 128), BF16),
            pltpu.VMEM((C_Z, ROWS, 128), BF16),
            pltpu.VMEM((C_Z, ROWS, 128), BF16),
            pltpu.VMEM((32, ROWS, RES), BF16),
            dma((4,)),
            dma((4,)), dma, dma((4,)), dma,
            dma((2, 8)), dma, dma((4,)), dma,
            dma((3, 4)), dma((3, 4)), dma((3, 4)), dma((3, 4)),
            dma((4, 4)), dma((4, 4)), dma((6,)), dma((6,)),
            dma, dma, dma, dma, dma((4,)), dma,
        ],
        compiler_params=pltpu.CompilerParams(
            collective_id=0, has_side_effects=True, vmem_limit_bytes=56 * 2**20
        ),
        cost_estimate=pl.CostEstimate(flops=12 * 10**9, bytes_accessed=8 * 2**20, transcendentals=10**6),
    )(msa, msa_mask, feat, coef, w2, wq, wout, mrow, mcol)


def body(
    homolog_embedding,
    alignment_mask,
    pairwise_features,
    residue_validity_mask,
    left_right_coefficients,
    outer_output_weight,
    triangle_input_weight,
    triangle_gate_weight,
    triangle_output_weight,
):
    w2 = jnp.transpose(outer_output_weight.reshape(LAT, LAT, C_Z), (2, 1, 0)).reshape(C_Z, LAT * LAT)
    wq = jnp.concatenate([triangle_input_weight, triangle_gate_weight[None]], 0)
    wq = jnp.transpose(wq, (0, 2, 1)).reshape(160, C_Z)
    return call(
        homolog_embedding, alignment_mask, pairwise_features, left_right_coefficients,
        w2, wq, triangle_output_weight.T,
        residue_validity_mask, residue_validity_mask.astype(F32).reshape(4, 128),
    )


def solution(mesh):
    return jax.shard_map(
        body,
        mesh=mesh,
        in_specs=(
            P(("dapw", "dapn"), None, None),
            P(("dapw", "dapn"), None),
            P("dapn", "dapw", None),
            P(),
            P(),
            P(),
            P(None, None, "dapn"),
            P(None, "dapn"),
            P(),
        ),
        out_specs=P("dapn", "dapw", None),
        check_vma=False,
    )
```

```python
import jax
import jax.numpy as jnp
from jax import lax
from jax.experimental import pallas as pl
from jax.experimental.pallas import tpu as pltpu
from jax.sharding import PartitionSpec as P

MESH = pl.DeviceIdType.MESH
BF16, F32 = jnp.bfloat16, jnp.float32
EPS = 1e-05
SEQS = 2048
RES = 512
C_Z = 128
LAT = 32
ROWS = 16
QUADS = 4


def position():
    w, n = lax.axis_index("dapw"), lax.axis_index("dapn")
    y, zh, x = w // 8, (w // 4) % 2, w % 4
    return y, zh * 2 + n // 2, x, n % 2


def at(y, z, x, k):
    return y * 8 + (z // 2) * 4 + x, (z % 2) * 2 + k


def block_of(y, z, k):
    return y * 8 + (z // 2) * 4 + k * 2 + z % 2


def remote(src, dst, send, recv, device):
    return pltpu.make_async_remote_copy(
        src_ref=src, dst_ref=dst, send_sem=send, recv_sem=recv, device_id=device, device_id_type=MESH
    )


def arrived(ref, sem):
    pltpu.make_async_copy(ref, ref, sem).wait()


def signal(sem, device):
    pl.semaphore_signal(sem, inc=1, device_id=device, device_id_type=MESH)


def lanes(start, size):
    return pl.ds(pl.multiple_of(start, size), size)


def kernel(
    msa, msa_mask, feat, coef, w_outer, w_edges, w_gate, w_out, mrow, mcol, out,
    held, lwide, rwide, left, right, w2wide, w2, wq, wout, lbuf, rbuf, lt, prod,
    z_opp, z_side, in_half, in_side, own, fbuf, wide, wfull,
    updated, normed, gate, outgoing, edges, tri, back, tile, landed,
    s_x, s_f, r_f, s_w, r_w, s_l1, r_l1, s_r1, r_r1, s_l2, r_l2, s_r2, r_r2, s_c, r_c,
    s_h, r_h, s_z, r_z, s_e, r_e, s_t, r_t, s_o, r_o,
):
    y, z, x, k = position()
    feature_z, feature_k = (z // 2) * 2 + x % 2, x // 2
    w, n = at(y, z, x, k)
    me = w * 4 + n
    yk = y * 2 + k
    ya, yb, yo = (y + 1) % 4, (y + 3) % 4, (y + 2) % 4
    xa, xb, xo = (x + 1) % 4, (x + 3) % 4, (x + 2) % 4
    za, zb, zo = (z + 1) % 4, (z + 3) % 4, (z + 2) % 4
    row_block = block_of(y, z, k)

    def load(g):
        part = pl.ds(g * 4, 4)
        return pltpu.make_async_copy(msa.at[part], held.at[part], s_x.at[g])

    for g in range(4):
        load(g).start()

    barrier = pltpu.get_barrier_semaphore()

    def greet(t, carry):
        o = (me + t) % 128
        signal(barrier, (o // 4, o % 4))
        return carry

    lax.fori_loop(1, 128, greet, 0)

    wl, wr = coef[:LAT], coef[LAT:]
    wide_coef = jnp.concatenate([wl] * 4 + [wr] * 4, axis=0).T
    column_sum = jnp.sum(wide_coef.astype(F32), 0, keepdims=True)
    mask_columns = msa_mask[...].astype(F32).T
    lane_part = lax.broadcasted_iota(jnp.int32, (1, 128), 1) // LAT
    for g in range(4):
        load(g).wait()
        packed = jnp.zeros((RES, 128), F32)
        for h in range(4):
            s = g * 4 + h
            values = held[s]
            v = values.astype(F32)
            center = jnp.sum(v, 1, keepdims=True) * (1.0 / 256)
            spread = jnp.sum(v * v, 1, keepdims=True) * (1.0 / 256) - center * center
            scale = lax.rsqrt(spread + EPS) * mask_columns[:, s : s + 1]
            mapped = jnp.dot(values, wide_coef, preferred_element_type=F32)
            mapped = (mapped - center * column_sum) * scale
            lefts = mapped[:, :128].reshape(16, 4, 8, 128)
            merged = lefts[:, 0]
            for rr in range(1, 4):
                merged = jnp.where(lane_part[None] == rr, lefts[:, rr], merged)
            lwide[s] = merged.reshape(128, 128)
            packed = jnp.where(lane_part == h, mapped[:, 128:], packed)
        rwide[g * 4 : (g + 1) * 4] = packed.T.reshape(4, LAT, RES)
    for t in range(128):
        left[:, t * 128 : (t + 1) * 128] = lwide[:, t, :].astype(BF16)
    for d in range(LAT):
        right[d] = rwide[:, d, :].astype(BF16)

    w2wide[...] = w_outer[...].astype(F32).reshape(LAT, LAT, C_Z)
    for d in range(0, LAT, 4):
        rows = jnp.concatenate([w2wide[:, d + h, :] for h in range(4)], axis=0)
        w2[:, d * LAT : (d + 4) * LAT] = rows.T.astype(BF16)
    wq[0:128] = w_edges[...]
    wq[128:160] = w_gate[...]
    wout[...] = w_out[...].T

    pl.semaphore_wait(barrier, 127)

    sends = []

    def push(src, dst, send, recv, device):
        copy = remote(src, dst, send, recv, device)
        copy.start()
        sends.append(copy)

    def left_block(o, h):
        return left.at[:, lanes((o // 2) * 4096 + h * 2048 + (o % 2) * 1024, 1024)]

    def half_of(p):
        return (z // 2 + 1 + p // 2) % 2

    for h in range(2):
        half = half_of(h * 2)
        target = lbuf.at[x, yk, :, lanes(half * 1024, 1024)]
        for t in range(1, 8):
            o = (yk + t) % 8
            push(left_block(o, half), target, s_l1.at[h, t], r_l1.at[h], at(o // 2, z, x, o % 2))
        pltpu.make_async_copy(left_block(yk, half), target, r_l1.at[h]).start()
        for q in (h * 2, h * 2 + 1):
            ds = pl.ds(q * 8, 8)
            target_r = rbuf.at[ds, x, yk]
            for t in range(1, 4):
                o = (x + t) % 4
                push(right.at[ds, :, lanes(o * 128, 128)], target_r, s_r1.at[q, t], r_r1.at[q], at(y, z, o, k))
            pltpu.make_async_copy(right.at[ds, :, lanes(x * 128, 128)], target_r, r_r1.at[q]).start()

    for t in range(1, 4):
        push(wq, wfull.at[n], s_w.at[t], r_w, (w, (n + t) % 4))
    pltpu.make_async_copy(wq, wfull.at[n], r_w).start()

    def feature_copy(t):
        tw, tn = at(y, feature_z, t, feature_k)
        return tw, tn, remote(
            feat.at[:, :, t * 128 : (t + 1) * 128], fbuf.at[pl.ds(n * 32, 32)], s_f.at[t], r_f, (tw, tn)
        )

    def left_part(slab, p):
        return lbuf.at[slab, (p % 2) * 4 : (p % 2) * 4 + 4, :, lanes(half_of(p) * 1024, 1024)]

    def right_part(yy, kk, q):
        return rbuf.at[q * 8 : (q + 1) * 8, :, yy * 2 + kk]

    for q in range(QUADS):
        if q % 2 == 0:
            arrived(lbuf.at[x, :, :, lanes(half_of(q) * 1024, 1024)], r_l1.at[q // 2])
            for p in (q, q + 1):
                push(left_part(x, p), left_part(x, p), s_l2.at[0, p], r_l2.at[0, p], at(y, z, xa, k))
                push(left_part(x, p), left_part(x, p), s_l2.at[1, p], r_l2.at[1, p], at(y, z, xb, k))
        arrived(rbuf.at[q * 8 : (q + 1) * 8, :, yk], r_r1.at[q])
        mine = right_part(y, k, q)
        push(mine, mine, s_r2.at[0, q], r_r2.at[0, q], at(ya, z, x, k))
        push(mine, mine, s_r2.at[1, q], r_r2.at[1, q], at(yb, z, x, k))
        push(mine, mine, s_c.at[0, q], r_c.at[0, q], at(y, z, x, 1 - k))

    def product(a, q):
        parts = [rbuf[q * 8 + h].reshape(512, 128) for h in range(8)]
        value = jnp.dot(lt[a], jnp.concatenate(parts, axis=1), preferred_element_type=F32).astype(BF16)
        for h in range(8):
            prod[pl.ds(a * 16, 16), pl.ds(pl.multiple_of((q * 8 + h) * 32, 32), 32), :] = value[
                :, h * 128 : (h + 1) * 128
            ].reshape(16, 32, 128)

    def products(half, q):
        lax.fori_loop(0, 2, lambda t, c: (product(half * 2 + t, q), c)[1], 0)

    def group_products(a):
        lax.fori_loop(0, 4, lambda q, c: (product(a, q), c)[1], 0)

    def means(a, part, store):
        rows = [prod[a * 16 + part * 8 + h] for h in range(8)]
        value = jnp.dot(w2[...], jnp.concatenate(rows, axis=1), preferred_element_type=F32) * (1.0 / SEQS)
        for h in range(8):
            store(part * 8 + h, value[:, h * 128 : (h + 1) * 128])

    for step in range(QUADS + 2):
        if step < QUADS:
            p = q = step
            for src, upward in ((yb, True), (ya, False)):
                part = right_part(src, k, q)
                arrived(part, r_r2.at[0 if upward else 1, q])
                if upward == (q % 2 == 0):
                    push(part, part, s_r2.at[2, q], r_r2.at[2, q], at(ya if upward else yb, z, x, k))
                side = 1 if upward else 2
                push(part, part, s_c.at[side, q], r_c.at[side, q], at(y, z, x, 1 - k))
            for src, upward in ((xb, True), (xa, False)):
                part = left_part(src, p)
                arrived(part, r_l2.at[0 if upward else 1, p])
                if upward == (p % 2 == 0):
                    push(part, part, s_l2.at[2, p], r_l2.at[2, p], at(y, z, xa if upward else xb, k))
        if 0 <= step - 1 < QUADS:
            p = q = step - 1
            part = right_part(yo, k, q)
            arrived(part, r_r2.at[2, q])
            push(part, part, s_c.at[3, q], r_c.at[3, q], at(y, z, x, 1 - k))
            arrived(left_part(xo, p), r_l2.at[2, p])
            if p % 2 == 1:
                half = half_of(p)
                turned = lbuf[:, :, :, lanes(half * 1024, 1024)].reshape(512, 1024).T
                for m in range(32):
                    zl, i = m // 16, m % 16
                    row = ((i % 8) * 4 + zl * 2 + i // 8) * 32
                    lt[half * 2 + zl, i * 32 : (i + 1) * 32] = turned[row : row + 32]
        if 0 <= step - 2:
            q = step - 2
            for side, src in ((0, y), (1, yb), (2, ya), (3, yo)):
                arrived(right_part(src, 1 - k, q), r_c.at[side, q])
            if q < QUADS - 1:
                products(half_of(0), q)

    for t in range(4):
        tw, tn, copy = feature_copy(t)

        @pl.when((tw != w) | (tn != n))
        def _():
            copy.start()

        @pl.when((tw == w) & (tn == n))
        def _():
            pltpu.make_async_copy(feat.at[:, :, t * 128 : (t + 1) * 128], fbuf.at[pl.ds(n * 32, 32)], r_f).start()

    def beyond(side):
        return (z + 1 + side * 2) % 4

    def store_opp(i, value):
        z_opp[i] = value.astype(BF16)

    def store_own(i, value):
        own[i] = value

    def send_side(side, part, turn, store):
        means(beyond(side), part, store)
        rows = pl.ds(pl.multiple_of(part * 8, 8), 8)
        push(
            z_side.at[side, rows], in_side.at[side, rows],
            s_z.at[side, turn], r_z.at[side, turn], at(y, beyond(side), x, k),
        )

    def send_early(side):
        def store(i, value):
            z_side[side, i] = value.astype(BF16)

        send_side(side, 1 - side, 0, store)

    def send_late(side):
        def store(i, value):
            z_side[side, i] = (value + in_half[side, i - side * 8].astype(F32)).astype(BF16)

        arrived(in_half.at[side], r_h.at[side])
        send_side(side, side, 1, store)

    product(zo, 3)
    for side in range(2):
        means(zo, side, store_opp)
        push(
            z_opp.at[side * 8 : side * 8 + 8], in_half.at[side],
            s_h.at[side], r_h.at[side], at(y, beyond(side), x, k),
        )
    far = 1 - z % 2
    product(beyond(far), 3)
    send_early(far)
    group_products(beyond(1 - far))
    send_early(1 - far)
    group_products(z)
    send_late(0)
    send_late(1)
    for part in range(2):
        means(z, part, store_own)

    arrived(fbuf, r_f)
    wide[0] = fbuf[...].astype(F32)
    for i in range(ROWS):
        own[i] = own[i] + wide[0, :, i, :]
    arrived(wfull, r_w)
    col_on = mcol[pl.ds(x, 1), :].astype(F32)
    for side in range(2):
        for turn in range(2):
            part = (1 - side) if turn == 0 else side
            arrived(in_side.at[side, part * 8 : part * 8 + 8], r_z.at[side, turn])
    for i in range(ROWS):
        total = (own[i] + in_side[0, i].astype(F32) + in_side[1, i].astype(F32)).astype(BF16)
        updated[i] = total
        u = total.astype(F32)
        center = jnp.sum(u, 0, keepdims=True) * (1.0 / C_Z)
        spread = jnp.sum(u * u, 0, keepdims=True) * (1.0 / C_Z) - center * center
        normed[i] = ((u - center) * lax.rsqrt(spread + EPS)).astype(BF16)

    def edge_quarter(t, carry):
        c = jnp.where(t == 3, y, (y + jnp.where(t == 0, 1, jnp.where(t == 1, 3, 2))) % 4)
        span = pl.ds(c * 32, 32)
        weights = wfull[c]
        for g in range(4):
            four = jnp.concatenate([normed[g * 4 + h] for h in range(4)], axis=1)
            proj = jnp.dot(weights, four, preferred_element_type=F32)
            for h in range(4):
                i = g * 4 + h
                p = proj[:, h * 128 : (h + 1) * 128]
                on = col_on * mrow[row_block * ROWS + i].astype(F32)
                wide[0, span, i, :] = jax.nn.sigmoid(p[0:32]) * p[32:64] * on
                wide[1, span, i, :] = jax.nn.sigmoid(p[64:96]) * p[96:128] * on
                gate[i, span, :] = p[128:160]
        for h in range(2):
            outgoing[span, h] = wide[h, span].astype(BF16)

        def send_edges(t, carry):
            o = c * 32 + (me + t * 11) % 32

            @pl.when(o != me)
            def _():
                remote(outgoing.at[o], edges.at[:, x, row_block], s_e, r_e, (o // 4, o % 4)).start()

            @pl.when(o == me)
            def _():
                pltpu.make_async_copy(outgoing.at[o], edges.at[:, x, row_block], r_e).start()

            return carry

        lax.fori_loop(0, 32, send_edges, 0)
        return carry

    lax.fori_loop(0, 4, edge_quarter, 0)
    gate[...] = jax.nn.sigmoid(gate[...])
    arrived(edges, r_e)

    first = jnp.concatenate([edges[0, b].reshape(RES, 128) for b in range(4)], axis=1)
    for q in (1, 3, 2, 0):
        b = (x + q) % 4
        second = jnp.concatenate(
            [edges[1, c, pl.ds(b * 8, 8)].reshape(128, 128) for c in range(4)], axis=1
        )
        value = lax.dot_general(first, second, (((1,), (1,)), ((), ())), preferred_element_type=F32)
        tri[b] = value.astype(BF16).reshape(32, ROWS, 128)

        def send_back(t, carry):
            r = (row_block + t * 11) % 32
            tw, tn = at(r // 8, ((r // 4) % 2) * 2 + r % 2, b, (r // 2) % 2)

            @pl.when((tw != w) | (tn != n))
            def _():
                remote(tri.at[b, r], back.at[me], s_t, r_t, (tw, tn)).start()

            @pl.when((tw == w) & (tn == n))
            def _():
                pltpu.make_async_copy(tri.at[b, r], back.at[me], r_t).start()

            return carry

        lax.fori_loop(0, 32, send_back, 0)

    arrived(back, r_t)
    wide[0] = back[...].astype(F32)
    for i in range(ROWS):
        t = wide[0, :, i, :]
        center = jnp.sum(t, 0, keepdims=True) * (1.0 / C_Z)
        spread = jnp.sum(t * t, 0, keepdims=True) * (1.0 / C_Z) - center * center
        normed[i] = ((t - center) * lax.rsqrt(spread + EPS)).astype(BF16)

    def out_parts(t):
        q = (x + (1, 3, 2, 0)[t]) % 4
        part = tile.at[pl.ds(q * 32, 32)]
        place = landed.at[:, :, lanes(x * 128, 128)]
        away = (row_block != w) | (n != q)
        return q, away, part, place, remote(part, place, s_o.at[t], r_o, (row_block, q))

    for t in range(4):
        q, away, part, place, copy = out_parts(t)
        span = pl.ds(pl.multiple_of(q * 32, 32), 32)
        for g in range(2):
            eight = jnp.concatenate([normed[g * 8 + h] for h in range(8)], axis=1)
            result = jnp.dot(wout[span, :], eight, preferred_element_type=F32)
            for h in range(8):
                i = g * 8 + h
                wide[1, span, i, :] = (
                    updated[i, span, :].astype(F32) + gate[i, span, :] * result[:, h * 128 : (h + 1) * 128]
                )
        tile[span] = wide[1, span].astype(BF16)

        @pl.when(away)
        def _():
            copy.start()

        @pl.when(jnp.logical_not(away))
        def _():
            pltpu.make_async_copy(part, place, r_o).start()

    arrived(landed, r_o)
    out[...] = landed[...]

    arrived(outgoing.at[0:127], s_e)
    arrived(back.at[0:127], s_t)
    for t in range(4):
        q, away, part, place, copy = out_parts(t)

        @pl.when(away)
        def _():
            copy.wait_send()

    for copy in sends:
        copy.wait_send()
    for t in range(4):
        tw, tn, copy = feature_copy(t)

        @pl.when((tw != w) | (tn != n))
        def _():
            copy.wait_send()


def call(*args):
    dma = pltpu.SemaphoreType.DMA
    vmem = pl.BlockSpec(memory_space=pltpu.VMEM)
    pair = pltpu.VMEM((ROWS, C_Z, 128), BF16)
    return pl.pallas_call(
        kernel,
        name="evoformer",
        out_shape=jax.ShapeDtypeStruct((32, ROWS, RES), BF16),
        in_specs=[pl.BlockSpec(memory_space=pl.ANY)]
        + [vmem] * 7
        + [pl.BlockSpec(memory_space=pltpu.SMEM), vmem],
        out_specs=vmem,
        scratch_shapes=[
            pltpu.VMEM((16, RES, 256), BF16),
            pltpu.VMEM((16, 128, 128), F32),
            pltpu.VMEM((16, LAT, RES), F32),
            pltpu.VMEM((16, RES * LAT), BF16),
            pltpu.VMEM((LAT, 16, RES), BF16),
            pltpu.VMEM((LAT, LAT, C_Z), F32),
            pltpu.VMEM((C_Z, LAT * LAT), BF16),
            pltpu.VMEM((160, C_Z), BF16),
            pltpu.VMEM((C_Z, C_Z), BF16),
            pltpu.VMEM((4, 8, 16, 2048), BF16),
            pltpu.VMEM((LAT, 4, 8, 16, 128), BF16),
            pltpu.VMEM((4, 512, 512), BF16),
            pltpu.VMEM((64, LAT * LAT, 128), BF16),
            pair,
            pltpu.VMEM((2, ROWS, C_Z, 128), BF16),
            pltpu.VMEM((2, 8, C_Z, 128), BF16),
            pltpu.VMEM((2, ROWS, C_Z, 128), BF16),
            pltpu.VMEM((ROWS, C_Z, 128), F32),
            pltpu.VMEM((C_Z, ROWS, 128), BF16),
            pltpu.VMEM((2, C_Z, ROWS, 128), F32),
            pltpu.VMEM((4, 160, C_Z), BF16),
            pair,
            pair,
            pltpu.VMEM((ROWS, C_Z, 128), F32),
            pltpu.VMEM((C_Z, 2, ROWS, 128), BF16),
            pltpu.VMEM((2, 4, 32, ROWS, 128), BF16),
            pltpu.VMEM((4, 32, ROWS, 128), BF16),
            pltpu.VMEM((C_Z, ROWS, 128), BF16),
            pltpu.VMEM((C_Z, ROWS, 128), BF16),
            pltpu.VMEM((32, ROWS, RES), BF16),
            dma((4,)),
            dma((4,)), dma, dma((4,)), dma,
            dma((2, 8)), dma((2,)), dma((4, 4)), dma((4,)),
            dma((3, 4)), dma((3, 4)), dma((3, 4)), dma((3, 4)),
            dma((4, 4)), dma((4, 4)),
            dma((2,)), dma((2,)), dma((2, 2)), dma((2, 2)),
            dma, dma, dma, dma, dma((4,)), dma,
        ],
        compiler_params=pltpu.CompilerParams(
            collective_id=0, has_side_effects=True, vmem_limit_bytes=52 * 2**20
        ),
        cost_estimate=pl.CostEstimate(flops=12 * 10**9, bytes_accessed=8 * 2**20, transcendentals=10**6),
    )(*args)


def body(
    homolog_embedding,
    alignment_mask,
    pairwise_features,
    residue_validity_mask,
    left_right_coefficients,
    outer_output_weight,
    triangle_input_weight,
    triangle_gate_weight,
    triangle_output_weight,
):
    edge_weights = jnp.transpose(triangle_input_weight, (0, 2, 1)).reshape(C_Z, C_Z)
    return call(
        homolog_embedding, alignment_mask, pairwise_features, left_right_coefficients.T,
        outer_output_weight, edge_weights, triangle_gate_weight.T, triangle_output_weight,
        residue_validity_mask, residue_validity_mask.reshape(4, 128),
    )


def solution(mesh):
    return jax.shard_map(
        body,
        mesh=mesh,
        in_specs=(
            P(("dapw", "dapn"), None, None),
            P(("dapw", "dapn"), None),
            P("dapn", "dapw", None),
            P(),
            P(),
            P(),
            P(None, None, "dapn"),
            P(None, "dapn"),
            P(),
        ),
        out_specs=P("dapn", "dapw", None),
        check_vma=False,
    )
```

```python
import jax
import jax.numpy as jnp
from jax import lax
from jax.experimental import pallas as pl
from jax.experimental.pallas import tpu as pltpu
from jax.sharding import PartitionSpec as P

MESH = pl.DeviceIdType.MESH
BF16, F32 = jnp.bfloat16, jnp.float32
EPS = 1e-05
SEQS = 2048
RES = 512
C_Z = 128
LAT = 32
ROWS = 16
QUADS = 4


def position():
    w, n = lax.axis_index("dapw"), lax.axis_index("dapn")
    y, zh, x = w // 8, (w // 4) % 2, w % 4
    return y, zh * 2 + n // 2, x, n % 2


def at(y, z, x, k):
    return y * 8 + (z // 2) * 4 + x, (z % 2) * 2 + k


def group_of(z, x):
    return (z // 2) * 2 + (z + x) % 2


def block_of(y, z, x, k):
    return y * 8 + (z // 2) * 4 + k * 2 + (z + x) % 2


def remote(src, dst, send, recv, device):
    return pltpu.make_async_remote_copy(
        src_ref=src, dst_ref=dst, send_sem=send, recv_sem=recv, device_id=device, device_id_type=MESH
    )


def arrived(ref, sem):
    pltpu.make_async_copy(ref, ref, sem).wait()


def signal(sem, device):
    pl.semaphore_signal(sem, inc=1, device_id=device, device_id_type=MESH)


def lanes(start, size):
    return pl.ds(pl.multiple_of(start, size), size)


def kernel(
    msa, msa_mask_hbm, feat, coef_hbm, w_outer_hbm, w_edges, w_gate, w_out_hbm, mrow, mcol_hbm, out,
    msa_mask, coef, w_outer, w_out, mcol,
    held, lwide, rwide, left, right, w2wide, w2, wq, wout, lbuf, rbuf, lt, prod,
    z_opp, z_side, in_half, in_side, own, fbuf, wide, wfull,
    updated, normed, gate, outgoing, edges, tri, back, tile, landed,
    s_x, s_i, s_f, r_f, s_w, r_w, s_l1, r_l1, s_r1, r_r1, s_l2, r_l2, s_r2, r_r2, s_c, r_c,
    s_h, r_h, s_z, r_z, s_e, r_e, s_t, r_t, s_o, r_o,
):
    y, z, x, k = position()
    w, n = at(y, z, x, k)
    me = w * 4 + n
    yk = y * 2 + k
    ya, yb, yo = (y + 1) % 4, (y + 3) % 4, (y + 2) % 4
    xa, xb, xo = (x + 1) % 4, (x + 3) % 4, (x + 2) % 4
    za, zb, zo = (z + 1) % 4, (z + 3) % 4, (z + 2) % 4
    row_block = block_of(y, z, x, k)

    def load(g):
        part = pl.ds(g * 4, 4)
        return pltpu.make_async_copy(msa.at[part], held.at[part], s_x.at[g])

    small = [
        pltpu.make_async_copy(src, dst, s_i.at[t])
        for t, (src, dst) in enumerate(
            (
                (coef_hbm, coef),
                (msa_mask_hbm, msa_mask),
                (w_outer_hbm, w_outer),
                (w_out_hbm, w_out),
                (mcol_hbm, mcol),
                (w_edges, wq.at[0:128]),
                (w_gate, wq.at[128:160]),
            )
        )
    ]
    small[0].start()
    small[1].start()
    for g in range(4):
        load(g).start()
    for copy in small[2:]:
        copy.start()

    barrier = pltpu.get_barrier_semaphore()

    def greet(t, carry):
        o = (me + t) % 128
        signal(barrier, (o // 4, o % 4))
        return carry

    lax.fori_loop(1, 128, greet, 0)

    small[0].wait()
    small[1].wait()
    wl, wr = coef[:LAT], coef[LAT:]
    wide_coef = jnp.concatenate([wl] * 4 + [wr] * 4, axis=0).T
    column_sum = jnp.sum(wide_coef.astype(F32), 0, keepdims=True)
    mask_columns = msa_mask[...].astype(F32).T
    lane_part = lax.broadcasted_iota(jnp.int32, (1, 128), 1) // LAT
    for g in range(4):
        load(g).wait()
        packed = jnp.zeros((RES, 128), F32)
        for h in range(4):
            s = g * 4 + h
            values = held[s]
            v = values.astype(F32)
            center = jnp.sum(v, 1, keepdims=True) * (1.0 / 256)
            spread = jnp.sum(v * v, 1, keepdims=True) * (1.0 / 256) - center * center
            scale = lax.rsqrt(spread + EPS) * mask_columns[:, s : s + 1]
            mapped = jnp.dot(values, wide_coef, preferred_element_type=F32)
            mapped = (mapped - center * column_sum) * scale
            lefts = mapped[:, :128].reshape(16, 4, 8, 128)
            merged = lefts[:, 0]
            for rr in range(1, 4):
                merged = jnp.where(lane_part[None] == rr, lefts[:, rr], merged)
            lwide[s] = merged.reshape(128, 128)
            packed = jnp.where(lane_part == h, mapped[:, 128:], packed)
        rwide[g * 4 : (g + 1) * 4] = packed.T.reshape(4, LAT, RES)
    for t in range(128):
        left[:, t * 128 : (t + 1) * 128] = lwide[:, t, :].astype(BF16)
    for d in range(LAT):
        right[d] = rwide[:, d, :].astype(BF16)

    for copy in small[2:]:
        copy.wait()
    w2wide[...] = w_outer[...].astype(F32).reshape(LAT, LAT, C_Z)
    for d in range(0, LAT, 4):
        rows = jnp.concatenate([w2wide[:, d + h, :] for h in range(4)], axis=0)
        w2[:, d * LAT : (d + 4) * LAT] = rows.T.astype(BF16)
    wout[...] = w_out[...].T

    pl.semaphore_wait(barrier, 127)

    sends = []

    def push(src, dst, send, recv, device):
        copy = remote(src, dst, send, recv, device)
        copy.start()
        sends.append(copy)

    def left_block(o, h):
        return left.at[:, lanes((o // 2) * 4096 + h * 2048 + (o % 2) * 1024, 1024)]

    def half_of(p):
        return (z // 2 + 1 + p // 2) % 2

    for h in range(2):
        half = half_of(h * 2)
        target = lbuf.at[x, yk, :, lanes(half * 1024, 1024)]
        for t in range(1, 8):
            o = (yk + t) % 8
            push(left_block(o, half), target, s_l1.at[h, t], r_l1.at[h], at(o // 2, z, x, o % 2))
        pltpu.make_async_copy(left_block(yk, half), target, r_l1.at[h]).start()
        for q in (h * 2, h * 2 + 1):
            ds = pl.ds(q * 8, 8)
            target_r = rbuf.at[ds, x, yk]
            for t in range(1, 4):
                o = (x + t) % 4
                push(right.at[ds, :, lanes(o * 128, 128)], target_r, s_r1.at[q, t], r_r1.at[q], at(y, z, o, k))
            pltpu.make_async_copy(right.at[ds, :, lanes(x * 128, 128)], target_r, r_r1.at[q]).start()

    for t in range(1, 4):
        push(wq, wfull.at[n], s_w.at[t], r_w, (w, (n + t) % 4))
    pltpu.make_async_copy(wq, wfull.at[n], r_w).start()

    def feature_copy(t):
        tw, tn = at(y, (z // 2) * 2 + (x + t) % 2, t, x // 2)
        return tw, tn, remote(
            feat.at[:, :, t * 128 : (t + 1) * 128], fbuf.at[pl.ds(n * 32, 32)], s_f.at[t], r_f, (tw, tn)
        )

    def left_part(slab, p):
        return lbuf.at[slab, (p % 2) * 4 : (p % 2) * 4 + 4, :, lanes(half_of(p) * 1024, 1024)]

    def right_part(yy, kk, q):
        return rbuf.at[q * 8 : (q + 1) * 8, :, yy * 2 + kk]

    def own_left(p):
        if p % 2 == 0:
            arrived(lbuf.at[x, :, :, lanes(half_of(p) * 1024, 1024)], r_l1.at[p // 2])
        push(left_part(x, p), left_part(x, p), s_l2.at[0, p], r_l2.at[0, p], at(y, z, xa, k))
        push(left_part(x, p), left_part(x, p), s_l2.at[1, p], r_l2.at[1, p], at(y, z, xb, k))

    def own_right(q):
        arrived(rbuf.at[q * 8 : (q + 1) * 8, :, yk], r_r1.at[q])
        mine = right_part(y, k, q)
        push(mine, mine, s_r2.at[0, q], r_r2.at[0, q], at(ya, z, x, k))
        push(mine, mine, s_r2.at[1, q], r_r2.at[1, q], at(yb, z, x, k))
        push(mine, mine, s_c.at[0, q], r_c.at[0, q], at(y, z, x, 1 - k))

    own_left(0)
    own_right(0)
    own_left(1)
    own_right(1)

    def product(a, q):
        parts = [rbuf[q * 8 + h].reshape(512, 128) for h in range(8)]
        value = jnp.dot(lt[a], jnp.concatenate(parts, axis=1), preferred_element_type=F32).astype(BF16)
        for h in range(8):
            prod[pl.ds(a * 16, 16), pl.ds(pl.multiple_of((q * 8 + h) * 32, 32), 32), :] = value[
                :, h * 128 : (h + 1) * 128
            ].reshape(16, 32, 128)

    def products(half, q):
        lax.fori_loop(0, 2, lambda t, c: (product(half * 2 + t, q), c)[1], 0)

    def group_products(a):
        lax.fori_loop(0, 4, lambda q, c: (product(a, q), c)[1], 0)

    def means(a, part, store):
        rows = [prod[a * 16 + part * 8 + h] for h in range(8)]
        value = jnp.dot(w2[...], jnp.concatenate(rows, axis=1), preferred_element_type=F32) * (1.0 / SEQS)
        for h in range(8):
            store(part * 8 + h, value[:, h * 128 : (h + 1) * 128])

    for step in range(QUADS + 2):
        if step < QUADS:
            p = q = step
            for src, upward in ((yb, True), (ya, False)):
                part = right_part(src, k, q)
                arrived(part, r_r2.at[0 if upward else 1, q])
                if upward == (q % 2 == 0):
                    push(part, part, s_r2.at[2, q], r_r2.at[2, q], at(ya if upward else yb, z, x, k))
                side = 1 if upward else 2
                push(part, part, s_c.at[side, q], r_c.at[side, q], at(y, z, x, 1 - k))
            for src, upward in ((xb, True), (xa, False)):
                part = left_part(src, p)
                arrived(part, r_l2.at[0 if upward else 1, p])
                if upward == (p % 2 == 0):
                    push(part, part, s_l2.at[2, p], r_l2.at[2, p], at(y, z, xa if upward else xb, k))
            if step + 2 < QUADS:
                own_left(step + 2)
                own_right(step + 2)
        if 0 <= step - 1 < QUADS:
            p = q = step - 1
            part = right_part(yo, k, q)
            arrived(part, r_r2.at[2, q])
            push(part, part, s_c.at[3, q], r_c.at[3, q], at(y, z, x, 1 - k))
            arrived(left_part(xo, p), r_l2.at[2, p])
            if p % 2 == 1:
                half = half_of(p)
                turned = lbuf[:, :, :, lanes(half * 1024, 1024)].reshape(512, 1024).T
                for m in range(32):
                    zl, i = m // 16, m % 16
                    row = ((i % 8) * 4 + zl * 2 + i // 8) * 32
                    lt[half * 2 + zl, i * 32 : (i + 1) * 32] = turned[row : row + 32]
        if 0 <= step - 2:
            q = step - 2
            for side, src in ((0, y), (1, yb), (2, ya), (3, yo)):
                arrived(right_part(src, 1 - k, q), r_c.at[side, q])
            if q < QUADS - 1:
                products(half_of(0), q)

    for t in range(4):
        tw, tn, copy = feature_copy(t)

        @pl.when((tw != w) | (tn != n))
        def _():
            copy.start()

        @pl.when((tw == w) & (tn == n))
        def _():
            pltpu.make_async_copy(feat.at[:, :, t * 128 : (t + 1) * 128], fbuf.at[pl.ds(n * 32, 32)], r_f).start()

    def beyond(side):
        return (z + 1 + side * 2) % 4

    def store_opp(i, value):
        z_opp[i] = value.astype(BF16)

    def store_own(i, value):
        own[i] = value

    def send_side(side, part, turn, store):
        means(group_of(beyond(side), x), part, store)
        rows = pl.ds(pl.multiple_of(part * 8, 8), 8)
        push(
            z_side.at[side, rows], in_side.at[side, rows],
            s_z.at[side, turn], r_z.at[side, turn], at(y, beyond(side), x, k),
        )

    def send_early(side):
        def store(i, value):
            z_side[side, i] = value.astype(BF16)

        send_side(side, 1 - side, 0, store)

    def send_late(side):
        def store(i, value):
            z_side[side, i] = (value + in_half[side, i - side * 8].astype(F32)).astype(BF16)

        arrived(in_half.at[side], r_h.at[side])
        send_side(side, side, 1, store)

    product(group_of(zo, x), 3)
    for side in range(2):
        means(group_of(zo, x), side, store_opp)
        push(
            z_opp.at[side * 8 : side * 8 + 8], in_half.at[side],
            s_h.at[side], r_h.at[side], at(y, beyond(side), x, k),
        )
    far = 1 - z % 2
    product(group_of(beyond(far), x), 3)
    send_early(far)
    group_products(group_of(beyond(1 - far), x))
    send_early(1 - far)
    group_products(group_of(z, x))
    send_late(0)
    send_late(1)
    for part in range(2):
        means(group_of(z, x), part, store_own)

    arrived(fbuf, r_f)
    wide[0] = fbuf[...].astype(F32)
    for i in range(ROWS):
        own[i] = own[i] + wide[0, :, i, :]
    arrived(wfull, r_w)
    col_on = mcol[pl.ds(x, 1), :].astype(F32)
    for side in range(2):
        for turn in range(2):
            part = (1 - side) if turn == 0 else side
            arrived(in_side.at[side, part * 8 : part * 8 + 8], r_z.at[side, turn])
    for i in range(ROWS):
        total = (own[i] + in_side[0, i].astype(F32) + in_side[1, i].astype(F32)).astype(BF16)
        updated[i] = total
        u = total.astype(F32)
        center = jnp.sum(u, 0, keepdims=True) * (1.0 / C_Z)
        spread = jnp.sum(u * u, 0, keepdims=True) * (1.0 / C_Z) - center * center
        normed[i] = ((u - center) * lax.rsqrt(spread + EPS)).astype(BF16)

    def edge_quarter(t, carry):
        c = jnp.where(t == 3, y, (y + jnp.where(t == 0, 1, jnp.where(t == 1, 3, 2))) % 4)
        span = pl.ds(c * 32, 32)
        weights = wfull[c]
        for g in range(4):
            four = jnp.concatenate([normed[g * 4 + h] for h in range(4)], axis=1)
            proj = jnp.dot(weights, four, preferred_element_type=F32)
            for h in range(4):
                i = g * 4 + h
                p = proj[:, h * 128 : (h + 1) * 128]
                on = col_on * mrow[row_block * ROWS + i].astype(F32)
                wide[0, span, i, :] = jax.nn.sigmoid(p[0:32]) * p[32:64] * on
                wide[1, span, i, :] = jax.nn.sigmoid(p[64:96]) * p[96:128] * on
                gate[i, span, :] = p[128:160]
        for h in range(2):
            outgoing[span, h] = wide[h, span].astype(BF16)

        def send_edges(t, carry):
            o = c * 32 + (me + t * 11) % 32

            @pl.when(o != me)
            def _():
                remote(outgoing.at[o], edges.at[:, x, row_block], s_e, r_e, (o // 4, o % 4)).start()

            @pl.when(o == me)
            def _():
                pltpu.make_async_copy(outgoing.at[o], edges.at[:, x, row_block], r_e).start()

            return carry

        lax.fori_loop(0, 32, send_edges, 0)
        return carry

    lax.fori_loop(0, 4, edge_quarter, 0)
    gate[...] = jax.nn.sigmoid(gate[...])
    arrived(edges, r_e)

    first = jnp.concatenate([edges[0, b].reshape(RES, 128) for b in range(4)], axis=1)
    for q in (1, 3, 2, 0):
        b = (x + q) % 4
        second = jnp.concatenate(
            [edges[1, c, pl.ds(b * 8, 8)].reshape(128, 128) for c in range(4)], axis=1
        )
        value = lax.dot_general(first, second, (((1,), (1,)), ((), ())), preferred_element_type=F32)
        tri[b] = value.astype(BF16).reshape(32, ROWS, 128)

        def send_back(t, carry):
            r = (row_block + t * 11) % 32
            tw, tn = at(r // 8, ((r // 4) % 2) * 2 + (r + b) % 2, b, (r // 2) % 2)

            @pl.when((tw != w) | (tn != n))
            def _():
                remote(tri.at[b, r], back.at[me], s_t, r_t, (tw, tn)).start()

            @pl.when((tw == w) & (tn == n))
            def _():
                pltpu.make_async_copy(tri.at[b, r], back.at[me], r_t).start()

            return carry

        lax.fori_loop(0, 32, send_back, 0)

    arrived(back, r_t)
    wide[0] = back[...].astype(F32)
    for i in range(ROWS):
        t = wide[0, :, i, :]
        center = jnp.sum(t, 0, keepdims=True) * (1.0 / C_Z)
        spread = jnp.sum(t * t, 0, keepdims=True) * (1.0 / C_Z) - center * center
        normed[i] = ((t - center) * lax.rsqrt(spread + EPS)).astype(BF16)

    def out_parts(t):
        q = (x + (1, 3, 2, 0)[t]) % 4
        part = tile.at[pl.ds(q * 32, 32)]
        place = landed.at[:, :, lanes(x * 128, 128)]
        away = (row_block != w) | (n != q)
        return q, away, part, place, remote(part, place, s_o.at[t], r_o, (row_block, q))

    for t in range(4):
        q, away, part, place, copy = out_parts(t)
        span = pl.ds(pl.multiple_of(q * 32, 32), 32)
        for g in range(2):
            eight = jnp.concatenate([normed[g * 8 + h] for h in range(8)], axis=1)
            result = jnp.dot(wout[span, :], eight, preferred_element_type=F32)
            for h in range(8):
                i = g * 8 + h
                wide[1, span, i, :] = (
                    updated[i, span, :].astype(F32) + gate[i, span, :] * result[:, h * 128 : (h + 1) * 128]
                )
        tile[span] = wide[1, span].astype(BF16)

        @pl.when(away)
        def _():
            copy.start()

        @pl.when(jnp.logical_not(away))
        def _():
            pltpu.make_async_copy(part, place, r_o).start()

    arrived(landed, r_o)
    out[...] = landed[...]

    arrived(outgoing.at[0:127], s_e)
    arrived(back.at[0:127], s_t)
    for t in range(4):
        q, away, part, place, copy = out_parts(t)

        @pl.when(away)
        def _():
            copy.wait_send()

    for copy in sends:
        copy.wait_send()
    for t in range(4):
        tw, tn, copy = feature_copy(t)

        @pl.when((tw != w) | (tn != n))
        def _():
            copy.wait_send()


def call(*args):
    dma = pltpu.SemaphoreType.DMA
    vmem = pl.BlockSpec(memory_space=pltpu.VMEM)
    hbm = pl.BlockSpec(memory_space=pltpu.HBM)
    pair = pltpu.VMEM((ROWS, C_Z, 128), BF16)
    return pl.pallas_call(
        kernel,
        name="evoformer",
        out_shape=jax.ShapeDtypeStruct((32, ROWS, RES), BF16),
        in_specs=[hbm] * 8 + [pl.BlockSpec(memory_space=pltpu.SMEM), hbm],
        out_specs=vmem,
        scratch_shapes=[
            pltpu.VMEM((16, RES), jnp.int32),
            pltpu.VMEM((2 * LAT, 256), BF16),
            pltpu.VMEM((LAT * LAT, C_Z), BF16),
            pltpu.VMEM((C_Z, C_Z), BF16),
            pltpu.VMEM((4, 128), jnp.int32),
            pltpu.VMEM((16, RES, 256), BF16),
            pltpu.VMEM((16, 128, 128), F32),
            pltpu.VMEM((16, LAT, RES), F32),
            pltpu.VMEM((16, RES * LAT), BF16),
            pltpu.VMEM((LAT, 16, RES), BF16),
            pltpu.VMEM((LAT, LAT, C_Z), F32),
            pltpu.VMEM((C_Z, LAT * LAT), BF16),
            pltpu.VMEM((160, C_Z), BF16),
            pltpu.VMEM((C_Z, C_Z), BF16),
            pltpu.VMEM((4, 8, 16, 2048), BF16),
            pltpu.VMEM((LAT, 4, 8, 16, 128), BF16),
            pltpu.VMEM((4, 512, 512), BF16),
            pltpu.VMEM((64, LAT * LAT, 128), BF16),
            pair,
            pltpu.VMEM((2, ROWS, C_Z, 128), BF16),
            pltpu.VMEM((2, 8, C_Z, 128), BF16),
            pltpu.VMEM((2, ROWS, C_Z, 128), BF16),
            pltpu.VMEM((ROWS, C_Z, 128), F32),
            pltpu.VMEM((C_Z, ROWS, 128), BF16),
            pltpu.VMEM((2, C_Z, ROWS, 128), F32),
            pltpu.VMEM((4, 160, C_Z), BF16),
            pair,
            pair,
            pltpu.VMEM((ROWS, C_Z, 128), F32),
            pltpu.VMEM((C_Z, 2, ROWS, 128), BF16),
            pltpu.VMEM((2, 4, 32, ROWS, 128), BF16),
            pltpu.VMEM((4, 32, ROWS, 128), BF16),
            pltpu.VMEM((C_Z, ROWS, 128), BF16),
            pltpu.VMEM((C_Z, ROWS, 128), BF16),
            pltpu.VMEM((32, ROWS, RES), BF16),
            dma((4,)), dma((7,)),
            dma((4,)), dma, dma((4,)), dma,
            dma((2, 8)), dma((2,)), dma((4, 4)), dma((4,)),
            dma((3, 4)), dma((3, 4)), dma((3, 4)), dma((3, 4)),
            dma((4, 4)), dma((4, 4)),
            dma((2,)), dma((2,)), dma((2, 2)), dma((2, 2)),
            dma, dma, dma, dma, dma((4,)), dma,
        ],
        compiler_params=pltpu.CompilerParams(
            collective_id=0, has_side_effects=True, vmem_limit_bytes=60 * 2**20
        ),
        cost_estimate=pl.CostEstimate(flops=12 * 10**9, bytes_accessed=8 * 2**20, transcendentals=10**6),
    )(*args)


def body(
    homolog_embedding,
    alignment_mask,
    pairwise_features,
    residue_validity_mask,
    left_right_coefficients,
    outer_output_weight,
    triangle_input_weight,
    triangle_gate_weight,
    triangle_output_weight,
):
    edge_weights = jnp.transpose(triangle_input_weight, (0, 2, 1)).reshape(C_Z, C_Z)
    return call(
        homolog_embedding, alignment_mask, pairwise_features, left_right_coefficients.T,
        outer_output_weight, edge_weights, triangle_gate_weight.T, triangle_output_weight,
        residue_validity_mask, residue_validity_mask.reshape(4, 128),
    )


def solution(mesh):
    return jax.shard_map(
        body,
        mesh=mesh,
        in_specs=(
            P(("dapw", "dapn"), None, None),
            P(("dapw", "dapn"), None),
            P("dapn", "dapw", None),
            P(),
            P(),
            P(),
            P(None, None, "dapn"),
            P(None, "dapn"),
            P(),
        ),
        out_specs=P("dapn", "dapw", None),
        check_vma=False,
    )
```

```python
import jax
import jax.numpy as jnp
from jax import lax
from jax.experimental import pallas as pl
from jax.experimental.pallas import tpu as pltpu
from jax.sharding import PartitionSpec as P

MESH = pl.DeviceIdType.MESH
BF16, F32 = jnp.bfloat16, jnp.float32
EPS = 1e-05
SEQS = 2048
RES = 512
C_Z = 128
LAT = 32
ROWS = 16
QUADS = 4


def position():
    w, n = lax.axis_index("dapw"), lax.axis_index("dapn")
    y, zh, x = w // 8, (w // 4) % 2, w % 4
    return y, zh * 2 + n // 2, x, n % 2


def at(y, z, x, k):
    return y * 8 + (z // 2) * 4 + x, (z % 2) * 2 + k


def group_of(z, x):
    return (z // 2) * 2 + (z + x) % 2


def block_of(y, z, x, k):
    return y * 8 + (z // 2) * 4 + k * 2 + (z + x) % 2


def remote(src, dst, send, recv, device):
    return pltpu.make_async_remote_copy(
        src_ref=src, dst_ref=dst, send_sem=send, recv_sem=recv, device_id=device, device_id_type=MESH
    )


def arrived(ref, sem):
    pltpu.make_async_copy(ref, ref, sem).wait()


def signal(sem, device):
    pl.semaphore_signal(sem, inc=1, device_id=device, device_id_type=MESH)


def lanes(start, size):
    return pl.ds(pl.multiple_of(start, size), size)


def kernel(
    msa, msa_mask_hbm, feat, coef_hbm, w_outer_hbm, w_edges, w_gate, w_out_hbm, mrow, mcol_hbm, out,
    msa_mask, coef, w_outer, w_out, mcol,
    held, lwide, rwide, left, right, w2wide, w2, wq, wout, lbuf, rbuf, lt, prod,
    z_opp, z_side, in_half, in_side, own, fhalf, fbuf, wide, wfull,
    updated, normed, gate, outgoing, edges, tri, back, tile,
    s_x, s_i, s_g, r_g, s_f, r_f, s_w, r_w, s_l1, r_l1, s_r1, r_r1, s_l2, r_l2, s_r2, r_r2, s_c, r_c,
    s_h, r_h, s_z, r_z, s_e, r_e, s_t, r_t, s_o, r_o,
):
    y, z, x, k = position()
    w, n = at(y, z, x, k)
    me = w * 4 + n
    yk = y * 2 + k
    ya, yb, yo = (y + 1) % 4, (y + 3) % 4, (y + 2) % 4
    xa, xb, xo = (x + 1) % 4, (x + 3) % 4, (x + 2) % 4
    za, zb, zo = (z + 1) % 4, (z + 3) % 4, (z + 2) % 4
    row_block = block_of(y, z, x, k)

    def load(g):
        part = pl.ds(g * 4, 4)
        return pltpu.make_async_copy(msa.at[part], held.at[part], s_x.at[g])

    small = [
        pltpu.make_async_copy(src, dst, s_i.at[t])
        for t, (src, dst) in enumerate(
            (
                (coef_hbm, coef),
                (msa_mask_hbm, msa_mask),
                (w_outer_hbm, w_outer),
                (w_out_hbm, w_out),
                (mcol_hbm, mcol),
                (w_edges, wq.at[0:128]),
                (w_gate, wq.at[128:160]),
            )
        )
    ]
    small[0].start()
    small[1].start()
    for g in range(4):
        load(g).start()
    for copy in small[2:]:
        copy.start()

    barrier = pltpu.get_barrier_semaphore()

    ws, ns = [(w + t) % 32 for t in range(32)], [(n + t) % 4 for t in range(4)]

    def greet(first, last):
        for t in range(first, last):
            signal(barrier, (ws[t // 4], ns[t % 4]))

    small[0].wait()
    small[1].wait()
    wl, wr = coef[:LAT], coef[LAT:]
    wide_coef = jnp.concatenate([wl] * 4 + [wr] * 4, axis=0).T
    column_sum = jnp.sum(wide_coef.astype(F32), 0, keepdims=True)
    mask_columns = msa_mask[...].astype(F32).T
    lane_part = lax.broadcasted_iota(jnp.int32, (1, 128), 1) // LAT
    for g in range(4):
        load(g).wait()
        packed = jnp.zeros((RES, 128), F32)
        for h in range(4):
            s = g * 4 + h
            if g == 0:
                greet(max(h * 32, 1), h * 32 + 32)
            values = held[s]
            v = values.astype(F32)
            center = jnp.sum(v, 1, keepdims=True) * (1.0 / 256)
            spread = jnp.sum(v * v, 1, keepdims=True) * (1.0 / 256) - center * center
            scale = lax.rsqrt(spread + EPS) * mask_columns[:, s : s + 1]
            mapped = jnp.dot(values, wide_coef, preferred_element_type=F32)
            mapped = (mapped - center * column_sum) * scale
            lefts = mapped[:, :128].reshape(16, 4, 8, 128)
            merged = lefts[:, 0]
            for rr in range(1, 4):
                merged = jnp.where(lane_part[None] == rr, lefts[:, rr], merged)
            lwide[s] = merged.reshape(128, 128)
            packed = jnp.where(lane_part == h, mapped[:, 128:], packed)
        rwide[g * 4 : (g + 1) * 4] = packed.T.reshape(4, LAT, RES)
    for t in range(128):
        left[:, t * 128 : (t + 1) * 128] = lwide[:, t, :].astype(BF16)
    for d in range(LAT):
        right[d] = rwide[:, d, :].astype(BF16)

    pl.semaphore_wait(barrier, 127)

    sends = []

    def push(src, dst, send, recv, device):
        copy = remote(src, dst, send, recv, device)
        copy.start()
        sends.append(copy)

    def left_block(o, h):
        return left.at[:, lanes((o // 2) * 4096 + h * 2048 + (o % 2) * 1024, 1024)]

    def half_of(p):
        return (z // 2 + 1 + p // 2) % 2

    for h in range(2):
        half = half_of(h * 2)
        target = lbuf.at[x, yk, :, lanes(half * 1024, 1024)]
        for t in range(1, 8):
            o = (yk + t) % 8
            push(left_block(o, half), target, s_l1.at[h, t], r_l1.at[h], at(o // 2, z, x, o % 2))
        pltpu.make_async_copy(left_block(yk, half), target, r_l1.at[h]).start()
        for q in (h * 2, h * 2 + 1):
            ds = pl.ds(q * 8, 8)
            target_r = rbuf.at[ds, x, yk]
            for t in range(1, 4):
                o = (x + t) % 4
                push(right.at[ds, :, lanes(o * 128, 128)], target_r, s_r1.at[q, t], r_r1.at[q], at(y, z, o, k))
            pltpu.make_async_copy(right.at[ds, :, lanes(x * 128, 128)], target_r, r_r1.at[q]).start()

    for copy in small[2:]:
        copy.wait()
    w2wide[...] = w_outer[...].astype(F32).reshape(LAT, LAT, C_Z)
    for d in range(0, LAT, 4):
        rows = jnp.concatenate([w2wide[:, d + h, :] for h in range(4)], axis=0)
        w2[:, d * LAT : (d + 4) * LAT] = rows.T.astype(BF16)
    wout[...] = w_out[...].T

    for t in range(1, 4):
        push(wq, wfull.at[n], s_w.at[t], r_w, (w, (n + t) % 4))
    pltpu.make_async_copy(wq, wfull.at[n], r_w).start()

    zl = z % 2
    partner = (1 - zl) * 2 + k
    for t in range(2):
        column = lanes(((x + 1 - zl + 2 * t) % 4) * 128, 128)
        push(feat.at[:, :, column], fhalf.at[t], s_g.at[t], r_g, (w, partner))

    def feature_copies(t):
        xt = (x + zl + 2 * t) % 4
        device = at(y, z, xt, x // 2)
        legs = ((feat.at[:, :, lanes(xt * 128, 128)], n), (fhalf.at[t], partner))
        places = [fbuf.at[pl.ds(pl.multiple_of(m * 32, 32), 32)] for _, m in legs]
        stays = (t == 0) & (zl == 0) & (k == x // 2)
        local = [pltpu.make_async_copy(src, dst, r_f) for (src, _), dst in zip(legs, places)]
        away = [
            remote(src, dst, s_f.at[t, h], r_f, device) for h, ((src, _), dst) in enumerate(zip(legs, places))
        ]
        return stays, local, away

    def left_part(slab, p):
        return lbuf.at[slab, (p % 2) * 4 : (p % 2) * 4 + 4, :, lanes(half_of(p) * 1024, 1024)]

    def right_part(yy, kk, q):
        return rbuf.at[q * 8 : (q + 1) * 8, :, yy * 2 + kk]

    def own_left(p):
        if p % 2 == 0:
            arrived(lbuf.at[x, :, :, lanes(half_of(p) * 1024, 1024)], r_l1.at[p // 2])
        push(left_part(x, p), left_part(x, p), s_l2.at[0, p], r_l2.at[0, p], at(y, z, xa, k))
        push(left_part(x, p), left_part(x, p), s_l2.at[1, p], r_l2.at[1, p], at(y, z, xb, k))

    def own_right(q):
        arrived(rbuf.at[q * 8 : (q + 1) * 8, :, yk], r_r1.at[q])
        mine = right_part(y, k, q)
        push(mine, mine, s_r2.at[0, q], r_r2.at[0, q], at(ya, z, x, k))
        push(mine, mine, s_r2.at[1, q], r_r2.at[1, q], at(yb, z, x, k))
        push(mine, mine, s_c.at[0, q], r_c.at[0, q], at(y, z, x, 1 - k))

    own_left(0)
    own_right(0)
    own_left(1)
    own_right(1)

    def product(a, q):
        parts = [rbuf[q * 8 + h].reshape(512, 128) for h in range(8)]
        value = jnp.dot(lt[a], jnp.concatenate(parts, axis=1), preferred_element_type=F32).astype(BF16)
        for h in range(8):
            prod[pl.ds(a * 16, 16), pl.ds(pl.multiple_of((q * 8 + h) * 32, 32), 32), :] = value[
                :, h * 128 : (h + 1) * 128
            ].reshape(16, 32, 128)

    def products(half, q):
        lax.fori_loop(0, 2, lambda t, c: (product(half * 2 + t, q), c)[1], 0)

    def group_products(a):
        lax.fori_loop(0, 4, lambda q, c: (product(a, q), c)[1], 0)

    def means(a, part, store):
        rows = [prod[a * 16 + part * 8 + h] for h in range(8)]
        value = jnp.dot(w2[...], jnp.concatenate(rows, axis=1), preferred_element_type=F32) * (1.0 / SEQS)
        for h in range(8):
            store(part * 8 + h, value[:, h * 128 : (h + 1) * 128])

    for step in range(QUADS + 2):
        if step < QUADS:
            p = q = step
            for src, upward in ((yb, True), (ya, False)):
                part = right_part(src, k, q)
                arrived(part, r_r2.at[0 if upward else 1, q])
                if upward == (q % 2 == 0):
                    push(part, part, s_r2.at[2, q], r_r2.at[2, q], at(ya if upward else yb, z, x, k))
                side = 1 if upward else 2
                push(part, part, s_c.at[side, q], r_c.at[side, q], at(y, z, x, 1 - k))
            for src, upward in ((xb, True), (xa, False)):
                part = left_part(src, p)
                arrived(part, r_l2.at[0 if upward else 1, p])
                if upward == (p % 2 == 0):
                    push(part, part, s_l2.at[2, p], r_l2.at[2, p], at(y, z, xa if upward else xb, k))
            if step + 2 < QUADS:
                own_left(step + 2)
                own_right(step + 2)
        if 0 <= step - 1 < QUADS:
            p = q = step - 1
            part = right_part(yo, k, q)
            arrived(part, r_r2.at[2, q])
            push(part, part, s_c.at[3, q], r_c.at[3, q], at(y, z, x, 1 - k))
            arrived(left_part(xo, p), r_l2.at[2, p])
            if p % 2 == 1:
                half = half_of(p)
                turned = lbuf[:, :, :, lanes(half * 1024, 1024)].reshape(512, 1024).T
                for m in range(32):
                    low, i = m // 16, m % 16
                    row = ((i % 8) * 4 + low * 2 + i // 8) * 32
                    lt[half * 2 + low, i * 32 : (i + 1) * 32] = turned[row : row + 32]
        if 0 <= step - 2:
            q = step - 2
            for side, src in ((0, y), (1, yb), (2, ya), (3, yo)):
                arrived(right_part(src, 1 - k, q), r_c.at[side, q])
            if q < QUADS - 1:
                products(half_of(0), q)

    arrived(fhalf, r_g)
    for t in range(2):
        stays, local, away = feature_copies(t)

        @pl.when(jnp.logical_not(stays))
        def _():
            for copy in away:
                copy.start()

        @pl.when(stays)
        def _():
            for copy in local:
                copy.start()

    def beyond(side):
        return (z + 1 + side * 2) % 4

    def store_opp(i, value):
        z_opp[i] = value.astype(BF16)

    def store_own(i, value):
        own[i] = value

    def send_side(side, part, turn, store):
        means(group_of(beyond(side), x), part, store)
        rows = pl.ds(pl.multiple_of(part * 8, 8), 8)
        push(
            z_side.at[side, rows], in_side.at[side, rows],
            s_z.at[side, turn], r_z.at[side, turn], at(y, beyond(side), x, k),
        )

    def send_early(side):
        def store(i, value):
            z_side[side, i] = value.astype(BF16)

        send_side(side, 1 - side, 0, store)

    def send_late(side):
        def store(i, value):
            z_side[side, i] = (value + in_half[side, i - side * 8].astype(F32)).astype(BF16)

        arrived(in_half.at[side], r_h.at[side])
        send_side(side, side, 1, store)

    product(group_of(zo, x), 3)
    for side in range(2):
        means(group_of(zo, x), side, store_opp)
        push(
            z_opp.at[side * 8 : side * 8 + 8], in_half.at[side],
            s_h.at[side], r_h.at[side], at(y, beyond(side), x, k),
        )
    far = 1 - z % 2
    product(group_of(beyond(far), x), 3)
    send_early(far)
    group_products(group_of(beyond(1 - far), x))
    send_early(1 - far)
    group_products(group_of(z, x))
    send_late(0)
    send_late(1)
    for part in range(2):
        means(group_of(z, x), part, store_own)

    arrived(fbuf, r_f)
    wide[0] = fbuf[...].astype(F32)
    for i in range(ROWS):
        own[i] = own[i] + wide[0, :, i, :]
    arrived(wfull, r_w)
    col_on = mcol[pl.ds(x, 1), :].astype(F32)
    for side in range(2):
        for turn in range(2):
            part = (1 - side) if turn == 0 else side
            arrived(in_side.at[side, part * 8 : part * 8 + 8], r_z.at[side, turn])
    for i in range(ROWS):
        total = (own[i] + in_side[0, i].astype(F32) + in_side[1, i].astype(F32)).astype(BF16)
        updated[i] = total
        u = total.astype(F32)
        center = jnp.sum(u, 0, keepdims=True) * (1.0 / C_Z)
        spread = jnp.sum(u * u, 0, keepdims=True) * (1.0 / C_Z) - center * center
        normed[i] = ((u - center) * lax.rsqrt(spread + EPS)).astype(BF16)

    def edge_quarter(c, first):
        span = pl.ds(c * 32, 32)
        weights = wfull[c, 0:128]
        for g in range(4):
            four = jnp.concatenate([normed[g * 4 + h] for h in range(4)], axis=1)
            proj = jnp.dot(weights, four, preferred_element_type=F32)
            for h in range(4):
                i = g * 4 + h
                p = proj[:, h * 128 : (h + 1) * 128]
                on = col_on * mrow[row_block * ROWS + i].astype(F32)
                wide[0, span, i, :] = jax.nn.sigmoid(p[0:32]) * p[32:64] * on
                wide[1, span, i, :] = jax.nn.sigmoid(p[64:96]) * p[96:128] * on
        for h in range(2):
            outgoing[span, h] = wide[h, span].astype(BF16)

        for t in range(first, 32):
            tw = c * 8 + lows[t // 4]
            tn = ns[t % 4]
            remote(outgoing.at[tw * 4 + tn], edges.at[:, x, row_block], s_e, r_e, (tw, tn)).start()

    lows = [((w // 4 + t % 2) % 2) * 4 + (x + t // 2) % 4 for t in range(8)]

    def far_quarter(t, carry):
        edge_quarter((y + jnp.where(t == 0, 2, 2 * t - 1)) % 4, 0)
        return carry

    lax.fori_loop(0, 3, far_quarter, 0)
    edge_quarter(y, 1)
    pltpu.make_async_copy(outgoing.at[me], edges.at[:, x, row_block], r_e).start()
    gate_weights = jnp.concatenate([wfull[c, 128:160] for c in range(4)], axis=0)
    for g in range(4):
        four = jnp.concatenate([normed[g * 4 + h] for h in range(4)], axis=1)
        opened = jax.nn.sigmoid(jnp.dot(gate_weights, four, preferred_element_type=F32))
        for h in range(4):
            gate[g * 4 + h] = opened[:, h * 128 : (h + 1) * 128]
    arrived(edges, r_e)

    first = jnp.concatenate([edges[0, b].reshape(RES, 128) for b in range(4)], axis=1)
    ys = [y, ya, yb, yo]
    hs, ls, ks = [z // 2, 1 - z // 2], [z % 2, 1 - z % 2], [k, 1 - k]
    for q in (1, 3, 2, 0):
        b = (x + q) % 4
        second = jnp.concatenate(
            [edges[1, c, pl.ds(b * 8, 8)].reshape(128, 128) for c in range(4)], axis=1
        )
        value = lax.dot_general(first, second, (((1,), (1,)), ((), ())), preferred_element_type=F32)
        tri[b] = value.astype(BF16).reshape(32, ROWS, 128)

        for t in range(32):
            ty, th, tl, tk = ys[t % 4], hs[(t // 4) % 2], ls[(t // 8) % 2], ks[t // 16]
            part = tri.at[b, ty * 8 + th * 4 + tk * 2 + (tl + b) % 2]
            if t or q:
                remote(part, back.at[me], s_t, r_t, (ty * 8 + th * 4 + b, tl * 2 + tk)).start()
            else:
                pltpu.make_async_copy(part, back.at[me], r_t).start()

    arrived(back, r_t)
    wide[0] = back[...].astype(F32)
    for i in range(ROWS):
        t = wide[0, :, i, :]
        center = jnp.sum(t, 0, keepdims=True) * (1.0 / C_Z)
        spread = jnp.sum(t * t, 0, keepdims=True) * (1.0 / C_Z) - center * center
        normed[i] = ((t - center) * lax.rsqrt(spread + EPS)).astype(BF16)

    def out_parts(t):
        q = (x + (1, 3, 2, 0)[t]) % 4
        part = tile.at[pl.ds(q * 32, 32)]
        place = out.at[:, :, lanes(x * 128, 128)]
        away = (row_block != w) | (n != q)
        return q, away, part, place, remote(part, place, s_o.at[t], r_o, (row_block, q))

    for t in range(4):
        q, away, part, place, copy = out_parts(t)
        span = pl.ds(pl.multiple_of(q * 32, 32), 32)
        for g in range(2):
            eight = jnp.concatenate([normed[g * 8 + h] for h in range(8)], axis=1)
            result = jnp.dot(wout[span, :], eight, preferred_element_type=F32)
            for h in range(8):
                i = g * 8 + h
                wide[1, span, i, :] = (
                    updated[i, span, :].astype(F32) + gate[i, span, :] * result[:, h * 128 : (h + 1) * 128]
                )
        tile[span] = wide[1, span].astype(BF16)

        @pl.when(away)
        def _():
            copy.start()

        @pl.when(jnp.logical_not(away))
        def _():
            pltpu.make_async_copy(part, place, r_o).start()

    arrived(out, r_o)

    arrived(outgoing.at[0:127], s_e)
    arrived(back.at[0:127], s_t)
    for t in range(4):
        q, away, part, place, copy = out_parts(t)

        @pl.when(away)
        def _():
            copy.wait_send()

    for copy in sends:
        copy.wait_send()
    for t in range(2):
        stays, local, away = feature_copies(t)

        @pl.when(jnp.logical_not(stays))
        def _():
            for copy in away:
                copy.wait_send()


def call(*args):
    dma = pltpu.SemaphoreType.DMA
    hbm = pl.BlockSpec(memory_space=pltpu.HBM)
    pair = pltpu.VMEM((ROWS, C_Z, 128), BF16)
    return pl.pallas_call(
        kernel,
        name="evoformer",
        out_shape=jax.ShapeDtypeStruct((32, ROWS, RES), BF16),
        in_specs=[hbm] * 8 + [pl.BlockSpec(memory_space=pltpu.SMEM), hbm],
        out_specs=hbm,
        scratch_shapes=[
            pltpu.VMEM((16, RES), jnp.int32),
            pltpu.VMEM((2 * LAT, 256), BF16),
            pltpu.VMEM((LAT * LAT, C_Z), BF16),
            pltpu.VMEM((C_Z, C_Z), BF16),
            pltpu.VMEM((4, 128), jnp.int32),
            pltpu.VMEM((16, RES, 256), BF16),
            pltpu.VMEM((16, 128, 128), F32),
            pltpu.VMEM((16, LAT, RES), F32),
            pltpu.VMEM((16, RES * LAT), BF16),
            pltpu.VMEM((LAT, 16, RES), BF16),
            pltpu.VMEM((LAT, LAT, C_Z), F32),
            pltpu.VMEM((C_Z, LAT * LAT), BF16),
            pltpu.VMEM((160, C_Z), BF16),
            pltpu.VMEM((C_Z, C_Z), BF16),
            pltpu.VMEM((4, 8, 16, 2048), BF16),
            pltpu.VMEM((LAT, 4, 8, 16, 128), BF16),
            pltpu.VMEM((4, 512, 512), BF16),
            pltpu.VMEM((64, LAT * LAT, 128), BF16),
            pair,
            pltpu.VMEM((2, ROWS, C_Z, 128), BF16),
            pltpu.VMEM((2, 8, C_Z, 128), BF16),
            pltpu.VMEM((2, ROWS, C_Z, 128), BF16),
            pltpu.VMEM((ROWS, C_Z, 128), F32),
            pltpu.VMEM((2, 32, ROWS, 128), BF16),
            pltpu.VMEM((C_Z, ROWS, 128), BF16),
            pltpu.VMEM((2, C_Z, ROWS, 128), F32),
            pltpu.VMEM((4, 160, C_Z), BF16),
            pair,
            pair,
            pltpu.VMEM((ROWS, C_Z, 128), F32),
            pltpu.VMEM((C_Z, 2, ROWS, 128), BF16),
            pltpu.VMEM((2, 4, 32, ROWS, 128), BF16),
            pltpu.VMEM((4, 32, ROWS, 128), BF16),
            pltpu.VMEM((C_Z, ROWS, 128), BF16),
            pltpu.VMEM((C_Z, ROWS, 128), BF16),
            dma((4,)), dma((7,)),
            dma((2,)), dma, dma((2, 2)), dma, dma((4,)), dma,
            dma((2, 8)), dma((2,)), dma((4, 4)), dma((4,)),
            dma((3, 4)), dma((3, 4)), dma((3, 4)), dma((3, 4)),
            dma((4, 4)), dma((4, 4)),
            dma((2,)), dma((2,)), dma((2, 2)), dma((2, 2)),
            dma, dma, dma, dma, dma((4,)), dma,
        ],
        compiler_params=pltpu.CompilerParams(
            collective_id=0, has_side_effects=True, vmem_limit_bytes=60 * 2**20
        ),
        cost_estimate=pl.CostEstimate(flops=12 * 10**9, bytes_accessed=8 * 2**20, transcendentals=10**6),
    )(*args)


def body(
    homolog_embedding,
    alignment_mask,
    pairwise_features,
    residue_validity_mask,
    left_right_coefficients,
    outer_output_weight,
    triangle_input_weight,
    triangle_gate_weight,
    triangle_output_weight,
):
    edge_weights = jnp.transpose(triangle_input_weight, (0, 2, 1)).reshape(C_Z, C_Z)
    return call(
        homolog_embedding, alignment_mask, pairwise_features, left_right_coefficients.T,
        outer_output_weight, edge_weights, triangle_gate_weight.T, triangle_output_weight,
        residue_validity_mask, residue_validity_mask.reshape(4, 128),
    )


def solution(mesh):
    return jax.shard_map(
        body,
        mesh=mesh,
        in_specs=(
            P(("dapw", "dapn"), None, None),
            P(("dapw", "dapn"), None),
            P("dapn", "dapw", None),
            P(),
            P(),
            P(),
            P(None, None, "dapn"),
            P(None, "dapn"),
            P(),
        ),
        out_specs=P("dapn", "dapw", None),
        check_vma=False,
    )
```

```python
import jax
import jax.numpy as jnp
from jax import lax
from jax.experimental import pallas as pl
from jax.experimental.pallas import tpu as pltpu
from jax.sharding import PartitionSpec as P

MESH = pl.DeviceIdType.MESH
BF16, F32 = jnp.bfloat16, jnp.float32
EPS = 1e-05
SEQS = 2048
RES = 512
C_Z = 128
LAT = 32
ROWS = 16
QUADS = 4


def position():
    w, n = lax.axis_index("dapw"), lax.axis_index("dapn")
    y, zh, x = w // 8, (w // 4) % 2, w % 4
    return y, zh * 2 + n // 2, x, n % 2


def at(y, z, x, k):
    return y * 8 + (z // 2) * 4 + x, (z % 2) * 2 + k


def group_of(z, x):
    return (z // 2) * 2 + (z + x) % 2


def block_of(y, z, x, k):
    return y * 8 + (z // 2) * 4 + k * 2 + (z + x) % 2


def remote(src, dst, send, recv, device):
    return pltpu.make_async_remote_copy(
        src_ref=src, dst_ref=dst, send_sem=send, recv_sem=recv, device_id=device, device_id_type=MESH
    )


def arrived(ref, sem):
    pltpu.make_async_copy(ref, ref, sem).wait()


def signal(sem, device):
    pl.semaphore_signal(sem, inc=1, device_id=device, device_id_type=MESH)


def lanes(start, size):
    return pl.ds(pl.multiple_of(start, size), size)


def kernel(
    msa, msa_mask_hbm, feat, coef_hbm, w_outer_hbm, w_edges, w_gate, w_out_hbm, mrow, mcol_hbm, out,
    msa_mask, coef, w_outer, w_out, mcol,
    held, lwide, rwide, left, right, w2wide, w2, wq, wout, lbuf, rbuf, lt, prod,
    z_opp, z_side, in_half, in_side, own, fhalf, fbuf, wide, wfull,
    updated, normed, gate, outgoing, edges, tri, back, tile,
    s_x, s_i, s_g, r_g, s_f, r_f, s_w, r_w, s_l1, r_l1, s_r1, r_r1, s_l2, r_l2, s_r2, r_r2, s_c, r_c,
    s_h, r_h, s_z, r_z, s_e, r_e, s_t, r_t, s_o, r_o,
):
    y, z, x, k = position()
    w, n = at(y, z, x, k)
    me = w * 4 + n
    yk = y * 2 + k
    ya, yb, yo = (y + 1) % 4, (y + 3) % 4, (y + 2) % 4
    xa, xb, xo = (x + 1) % 4, (x + 3) % 4, (x + 2) % 4
    za, zb, zo = (z + 1) % 4, (z + 3) % 4, (z + 2) % 4
    row_block = block_of(y, z, x, k)

    def load(g):
        part = pl.ds(g * 4, 4)
        return pltpu.make_async_copy(msa.at[part], held.at[part], s_x.at[g])

    small = [
        pltpu.make_async_copy(src, dst, s_i.at[t])
        for t, (src, dst) in enumerate(
            (
                (coef_hbm, coef),
                (msa_mask_hbm, msa_mask),
                (w_outer_hbm, w_outer),
                (w_out_hbm, w_out),
                (mcol_hbm, mcol),
                (w_edges, wq.at[0:128]),
                (w_gate, wq.at[128:160]),
            )
        )
    ]
    small[0].start()
    small[1].start()
    for g in range(4):
        load(g).start()
    for copy in small[2:]:
        copy.start()

    barrier = pltpu.get_barrier_semaphore()

    ws, ns = [(w + t) % 32 for t in range(32)], [(n + t) % 4 for t in range(4)]

    def greet(first, last):
        for t in range(first, last):
            signal(barrier, (ws[t // 4], ns[t % 4]))

    greet(1, 128)
    small[0].wait()
    small[1].wait()
    wl, wr = coef[:LAT], coef[LAT:]
    wide_coef = jnp.concatenate([wl] * 4 + [wr] * 4, axis=0).T
    column_sum = jnp.sum(wide_coef.astype(F32), 0, keepdims=True)
    mask_columns = msa_mask[...].astype(F32).T
    lane_part = lax.broadcasted_iota(jnp.int32, (1, 128), 1) // LAT
    for g in range(4):
        load(g).wait()
        packed = jnp.zeros((RES, 128), F32)
        for h in range(4):
            s = g * 4 + h
            values = held[s]
            v = values.astype(F32)
            center = jnp.sum(v, 1, keepdims=True) * (1.0 / 256)
            spread = jnp.sum(v * v, 1, keepdims=True) * (1.0 / 256) - center * center
            scale = lax.rsqrt(spread + EPS) * mask_columns[:, s : s + 1]
            mapped = jnp.dot(values, wide_coef, preferred_element_type=F32)
            mapped = (mapped - center * column_sum) * scale
            lefts = mapped[:, :128].reshape(16, 4, 8, 128)
            merged = lefts[:, 0]
            for rr in range(1, 4):
                merged = jnp.where(lane_part[None] == rr, lefts[:, rr], merged)
            lwide[s] = merged.reshape(128, 128)
            packed = jnp.where(lane_part == h, mapped[:, 128:], packed)
        rwide[g * 4 : (g + 1) * 4] = packed.T.reshape(4, LAT, RES)
    for t in range(128):
        left[:, t * 128 : (t + 1) * 128] = lwide[:, t, :].astype(BF16)
    for d in range(LAT):
        right[d] = rwide[:, d, :].astype(BF16)

    pl.semaphore_wait(barrier, 127)

    sends = []

    def push(src, dst, send, recv, device):
        copy = remote(src, dst, send, recv, device)
        copy.start()
        sends.append(copy)

    def left_block(o, h):
        return left.at[:, lanes((o // 2) * 4096 + h * 2048 + (o % 2) * 1024, 1024)]

    def half_of(p):
        return (z // 2 + 1 + p // 2) % 2

    for h in range(2):
        half = half_of(h * 2)
        target = lbuf.at[x, yk, :, lanes(half * 1024, 1024)]
        for t in range(1, 8):
            o = (yk + t) % 8
            push(left_block(o, half), target, s_l1.at[h, t], r_l1.at[h], at(o // 2, z, x, o % 2))
        pltpu.make_async_copy(left_block(yk, half), target, r_l1.at[h]).start()
        for q in (h * 2, h * 2 + 1):
            ds = pl.ds(q * 8, 8)
            target_r = rbuf.at[ds, x, yk]
            for t in range(1, 4):
                o = (x + t) % 4
                push(right.at[ds, :, lanes(o * 128, 128)], target_r, s_r1.at[q, t], r_r1.at[q], at(y, z, o, k))
            pltpu.make_async_copy(right.at[ds, :, lanes(x * 128, 128)], target_r, r_r1.at[q]).start()

    for copy in small[2:]:
        copy.wait()
    w2wide[...] = w_outer[...].astype(F32).reshape(LAT, LAT, C_Z)
    for d in range(0, LAT, 4):
        rows = jnp.concatenate([w2wide[:, d + h, :] for h in range(4)], axis=0)
        w2[:, d * LAT : (d + 4) * LAT] = rows.T.astype(BF16)
    wout[...] = w_out[...].T

    for t in range(1, 4):
        push(wq, wfull.at[n], s_w.at[t], r_w, (w, (n + t) % 4))
    pltpu.make_async_copy(wq, wfull.at[n], r_w).start()

    zl = z % 2
    partner = (1 - zl) * 2 + k
    for t in range(2):
        column = lanes(((x + 1 - zl + 2 * t) % 4) * 128, 128)
        push(feat.at[:, :, column], fhalf.at[t], s_g.at[t], r_g, (w, partner))

    def feature_copies(t):
        xt = (x + zl + 2 * t) % 4
        device = at(y, z, xt, x // 2)
        legs = ((feat.at[:, :, lanes(xt * 128, 128)], n), (fhalf.at[t], partner))
        places = [fbuf.at[pl.ds(pl.multiple_of(m * 32, 32), 32)] for _, m in legs]
        stays = (t == 0) & (zl == 0) & (k == x // 2)
        local = [pltpu.make_async_copy(src, dst, r_f) for (src, _), dst in zip(legs, places)]
        away = [
            remote(src, dst, s_f.at[t, h], r_f, device) for h, ((src, _), dst) in enumerate(zip(legs, places))
        ]
        return stays, local, away

    def left_part(slab, p):
        return lbuf.at[slab, (p % 2) * 4 : (p % 2) * 4 + 4, :, lanes(half_of(p) * 1024, 1024)]

    def right_part(yy, kk, q):
        return rbuf.at[q * 8 : (q + 1) * 8, :, yy * 2 + kk]

    def own_left(p):
        if p % 2 == 0:
            arrived(lbuf.at[x, :, :, lanes(half_of(p) * 1024, 1024)], r_l1.at[p // 2])
        push(left_part(x, p), left_part(x, p), s_l2.at[0, p], r_l2.at[0, p], at(y, z, xa, k))
        push(left_part(x, p), left_part(x, p), s_l2.at[1, p], r_l2.at[1, p], at(y, z, xb, k))

    def own_right(q):
        arrived(rbuf.at[q * 8 : (q + 1) * 8, :, yk], r_r1.at[q])
        mine = right_part(y, k, q)
        push(mine, mine, s_r2.at[0, q], r_r2.at[0, q], at(ya, z, x, k))
        push(mine, mine, s_r2.at[1, q], r_r2.at[1, q], at(yb, z, x, k))
        push(mine, mine, s_c.at[0, q], r_c.at[0, q], at(y, z, x, 1 - k))

    own_left(0)
    own_right(0)
    own_left(1)
    own_right(1)

    def product(a, q):
        parts = [rbuf[q * 8 + h].reshape(512, 128) for h in range(8)]
        value = jnp.dot(lt[a], jnp.concatenate(parts, axis=1), preferred_element_type=F32).astype(BF16)
        for h in range(8):
            prod[pl.ds(a * 16, 16), pl.ds(pl.multiple_of((q * 8 + h) * 32, 32), 32), :] = value[
                :, h * 128 : (h + 1) * 128
            ].reshape(16, 32, 128)

    def products(half, q):
        lax.fori_loop(0, 2, lambda t, c: (product(half * 2 + t, q), c)[1], 0)

    def group_products(a):
        lax.fori_loop(0, 4, lambda q, c: (product(a, q), c)[1], 0)

    def means(a, part, store):
        rows = [prod[a * 16 + part * 8 + h] for h in range(8)]
        value = jnp.dot(w2[...], jnp.concatenate(rows, axis=1), preferred_element_type=F32) * (1.0 / SEQS)
        for h in range(8):
            store(part * 8 + h, value[:, h * 128 : (h + 1) * 128])

    for step in range(QUADS + 2):
        if step < QUADS:
            p = q = step
            for src, upward in ((yb, True), (ya, False)):
                part = right_part(src, k, q)
                arrived(part, r_r2.at[0 if upward else 1, q])
                if upward == (q % 2 == 0):
                    push(part, part, s_r2.at[2, q], r_r2.at[2, q], at(ya if upward else yb, z, x, k))
                side = 1 if upward else 2
                push(part, part, s_c.at[side, q], r_c.at[side, q], at(y, z, x, 1 - k))
            for src, upward in ((xb, True), (xa, False)):
                part = left_part(src, p)
                arrived(part, r_l2.at[0 if upward else 1, p])
                if upward == (p % 2 == 0):
                    push(part, part, s_l2.at[2, p], r_l2.at[2, p], at(y, z, xa if upward else xb, k))
            if step + 2 < QUADS:
                own_left(step + 2)
                own_right(step + 2)
        if 0 <= step - 1 < QUADS:
            p = q = step - 1
            part = right_part(yo, k, q)
            arrived(part, r_r2.at[2, q])
            push(part, part, s_c.at[3, q], r_c.at[3, q], at(y, z, x, 1 - k))
            arrived(left_part(xo, p), r_l2.at[2, p])
            if p % 2 == 1:
                half = half_of(p)
                turned = lbuf[:, :, :, lanes(half * 1024, 1024)].reshape(512, 1024).T
                for m in range(32):
                    low, i = m // 16, m % 16
                    row = ((i % 8) * 4 + low * 2 + i // 8) * 32
                    lt[half * 2 + low, i * 32 : (i + 1) * 32] = turned[row : row + 32]
        if 0 <= step - 2:
            q = step - 2
            for side, src in ((0, y), (1, yb), (2, ya), (3, yo)):
                arrived(right_part(src, 1 - k, q), r_c.at[side, q])
            if q < QUADS - 1:
                products(half_of(0), q)

    arrived(fhalf, r_g)
    for t in range(2):
        stays, local, away = feature_copies(t)

        @pl.when(jnp.logical_not(stays))
        def _():
            for copy in away:
                copy.start()

        @pl.when(stays)
        def _():
            for copy in local:
                copy.start()

    def beyond(side):
        return (z + 1 + side * 2) % 4

    def store_opp(i, value):
        z_opp[i] = value.astype(BF16)

    def store_own(i, value):
        own[i] = value

    def send_side(side, part, turn, store):
        means(group_of(beyond(side), x), part, store)
        rows = pl.ds(pl.multiple_of(part * 8, 8), 8)
        push(
            z_side.at[side, rows], in_side.at[side, rows],
            s_z.at[side, turn], r_z.at[side, turn], at(y, beyond(side), x, k),
        )

    def send_early(side):
        def store(i, value):
            z_side[side, i] = value.astype(BF16)

        send_side(side, 1 - side, 0, store)

    def send_late(side):
        def store(i, value):
            z_side[side, i] = (value + in_half[side, i - side * 8].astype(F32)).astype(BF16)

        arrived(in_half.at[side], r_h.at[side])
        send_side(side, side, 1, store)

    product(group_of(zo, x), 3)
    for side in range(2):
        means(group_of(zo, x), side, store_opp)
        push(
            z_opp.at[side * 8 : side * 8 + 8], in_half.at[side],
            s_h.at[side], r_h.at[side], at(y, beyond(side), x, k),
        )
    far = 1 - z % 2
    product(group_of(beyond(far), x), 3)
    send_early(far)
    group_products(group_of(beyond(1 - far), x))
    send_early(1 - far)
    group_products(group_of(z, x))
    send_late(0)
    send_late(1)
    for part in range(2):
        means(group_of(z, x), part, store_own)

    arrived(fbuf, r_f)
    wide[0] = fbuf[...].astype(F32)
    for i in range(ROWS):
        own[i] = own[i] + wide[0, :, i, :]
    arrived(wfull, r_w)
    col_on = mcol[pl.ds(x, 1), :].astype(F32)
    for side in range(2):
        for turn in range(2):
            part = (1 - side) if turn == 0 else side
            arrived(in_side.at[side, part * 8 : part * 8 + 8], r_z.at[side, turn])
    for i in range(ROWS):
        total = (own[i] + in_side[0, i].astype(F32) + in_side[1, i].astype(F32)).astype(BF16)
        updated[i] = total
        u = total.astype(F32)
        center = jnp.sum(u, 0, keepdims=True) * (1.0 / C_Z)
        spread = jnp.sum(u * u, 0, keepdims=True) * (1.0 / C_Z) - center * center
        normed[i] = ((u - center) * lax.rsqrt(spread + EPS)).astype(BF16)

    def edge_quarter(c, first):
        span = pl.ds(c * 32, 32)
        weights = wfull[c, 0:128]
        for g in range(4):
            four = jnp.concatenate([normed[g * 4 + h] for h in range(4)], axis=1)
            proj = jnp.dot(weights, four, preferred_element_type=F32)
            for h in range(4):
                i = g * 4 + h
                p = proj[:, h * 128 : (h + 1) * 128]
                on = col_on * mrow[row_block * ROWS + i].astype(F32)
                wide[0, span, i, :] = jax.nn.sigmoid(p[0:32]) * p[32:64] * on
                wide[1, span, i, :] = jax.nn.sigmoid(p[64:96]) * p[96:128] * on
        for h in range(2):
            outgoing[span, h] = wide[h, span].astype(BF16)

        for t in range(first, 32):
            tw = c * 8 + lows[t // 4]
            tn = ns[t % 4]
            remote(outgoing.at[tw * 4 + tn], edges.at[:, x, row_block], s_e, r_e, (tw, tn)).start()

    lows = [((w // 4 + t % 2) % 2) * 4 + (x + t // 2) % 4 for t in range(8)]

    def far_quarter(t, carry):
        edge_quarter((y + jnp.where(t == 0, 2, 2 * t - 1)) % 4, 0)
        return carry

    lax.fori_loop(0, 3, far_quarter, 0)
    edge_quarter(y, 1)
    pltpu.make_async_copy(outgoing.at[me], edges.at[:, x, row_block], r_e).start()
    gate_weights = jnp.concatenate([wfull[c, 128:160] for c in range(4)], axis=0)
    for g in range(4):
        four = jnp.concatenate([normed[g * 4 + h] for h in range(4)], axis=1)
        opened = jax.nn.sigmoid(jnp.dot(gate_weights, four, preferred_element_type=F32))
        for h in range(4):
            gate[g * 4 + h] = opened[:, h * 128 : (h + 1) * 128]
    arrived(edges, r_e)

    first = jnp.concatenate([edges[0, b].reshape(RES, 128) for b in range(4)], axis=1)
    ys = [y, ya, yb, yo]
    hs, ls, ks = [z // 2, 1 - z // 2], [z % 2, 1 - z % 2], [k, 1 - k]
    for q in (1, 3, 2, 0):
        b = (x + q) % 4
        second = jnp.concatenate(
            [edges[1, c, pl.ds(b * 8, 8)].reshape(128, 128) for c in range(4)], axis=1
        )
        value = lax.dot_general(first, second, (((1,), (1,)), ((), ())), preferred_element_type=F32)
        tri[b] = value.astype(BF16).reshape(32, ROWS, 128)

        for t in range(32):
            ty, th, tl, tk = ys[t % 4], hs[(t // 4) % 2], ls[(t // 8) % 2], ks[t // 16]
            part = tri.at[b, ty * 8 + th * 4 + tk * 2 + (tl + b) % 2]
            if t or q:
                remote(part, back.at[me], s_t, r_t, (ty * 8 + th * 4 + b, tl * 2 + tk)).start()
            else:
                pltpu.make_async_copy(part, back.at[me], r_t).start()

    arrived(back, r_t)
    wide[0] = back[...].astype(F32)
    for i in range(ROWS):
        t = wide[0, :, i, :]
        center = jnp.sum(t, 0, keepdims=True) * (1.0 / C_Z)
        spread = jnp.sum(t * t, 0, keepdims=True) * (1.0 / C_Z) - center * center
        normed[i] = ((t - center) * lax.rsqrt(spread + EPS)).astype(BF16)

    def out_parts(t):
        q = (x + (1, 3, 2, 0)[t]) % 4
        part = tile.at[pl.ds(q * 32, 32)]
        place = out.at[:, :, lanes(x * 128, 128)]
        away = (row_block != w) | (n != q)
        return q, away, part, place, remote(part, place, s_o.at[t], r_o, (row_block, q))

    for t in range(4):
        q, away, part, place, copy = out_parts(t)
        span = pl.ds(pl.multiple_of(q * 32, 32), 32)
        for g in range(2):
            eight = jnp.concatenate([normed[g * 8 + h] for h in range(8)], axis=1)
            result = jnp.dot(wout[span, :], eight, preferred_element_type=F32)
            for h in range(8):
                i = g * 8 + h
                wide[1, span, i, :] = (
                    updated[i, span, :].astype(F32) + gate[i, span, :] * result[:, h * 128 : (h + 1) * 128]
                )
        tile[span] = wide[1, span].astype(BF16)

        @pl.when(away)
        def _():
            copy.start()

        @pl.when(jnp.logical_not(away))
        def _():
            pltpu.make_async_copy(part, place, r_o).start()

    arrived(out, r_o)

    arrived(outgoing.at[0:127], s_e)
    arrived(back.at[0:127], s_t)
    for t in range(4):
        q, away, part, place, copy = out_parts(t)

        @pl.when(away)
        def _():
            copy.wait_send()

    for copy in sends:
        copy.wait_send()
    for t in range(2):
        stays, local, away = feature_copies(t)

        @pl.when(jnp.logical_not(stays))
        def _():
            for copy in away:
                copy.wait_send()


def call(*args):
    dma = pltpu.SemaphoreType.DMA
    hbm = pl.BlockSpec(memory_space=pltpu.HBM)
    pair = pltpu.VMEM((ROWS, C_Z, 128), BF16)
    return pl.pallas_call(
        kernel,
        name="evoformer",
        out_shape=jax.ShapeDtypeStruct((32, ROWS, RES), BF16),
        in_specs=[hbm] * 8 + [pl.BlockSpec(memory_space=pltpu.SMEM), hbm],
        out_specs=hbm,
        scratch_shapes=[
            pltpu.VMEM((16, RES), jnp.int32),
            pltpu.VMEM((2 * LAT, 256), BF16),
            pltpu.VMEM((LAT * LAT, C_Z), BF16),
            pltpu.VMEM((C_Z, C_Z), BF16),
            pltpu.VMEM((4, 128), jnp.int32),
            pltpu.VMEM((16, RES, 256), BF16),
            pltpu.VMEM((16, 128, 128), F32),
            pltpu.VMEM((16, LAT, RES), F32),
            pltpu.VMEM((16, RES * LAT), BF16),
            pltpu.VMEM((LAT, 16, RES), BF16),
            pltpu.VMEM((LAT, LAT, C_Z), F32),
            pltpu.VMEM((C_Z, LAT * LAT), BF16),
            pltpu.VMEM((160, C_Z), BF16),
            pltpu.VMEM((C_Z, C_Z), BF16),
            pltpu.VMEM((4, 8, 16, 2048), BF16),
            pltpu.VMEM((LAT, 4, 8, 16, 128), BF16),
            pltpu.VMEM((4, 512, 512), BF16),
            pltpu.VMEM((64, LAT * LAT, 128), BF16),
            pair,
            pltpu.VMEM((2, ROWS, C_Z, 128), BF16),
            pltpu.VMEM((2, 8, C_Z, 128), BF16),
            pltpu.VMEM((2, ROWS, C_Z, 128), BF16),
            pltpu.VMEM((ROWS, C_Z, 128), F32),
            pltpu.VMEM((2, 32, ROWS, 128), BF16),
            pltpu.VMEM((C_Z, ROWS, 128), BF16),
            pltpu.VMEM((2, C_Z, ROWS, 128), F32),
            pltpu.VMEM((4, 160, C_Z), BF16),
            pair,
            pair,
            pltpu.VMEM((ROWS, C_Z, 128), F32),
            pltpu.VMEM((C_Z, 2, ROWS, 128), BF16),
            pltpu.VMEM((2, 4, 32, ROWS, 128), BF16),
            pltpu.VMEM((4, 32, ROWS, 128), BF16),
            pltpu.VMEM((C_Z, ROWS, 128), BF16),
            pltpu.VMEM((C_Z, ROWS, 128), BF16),
            dma((4,)), dma((7,)),
            dma((2,)), dma, dma((2, 2)), dma, dma((4,)), dma,
            dma((2, 8)), dma((2,)), dma((4, 4)), dma((4,)),
            dma((3, 4)), dma((3, 4)), dma((3, 4)), dma((3, 4)),
            dma((4, 4)), dma((4, 4)),
            dma((2,)), dma((2,)), dma((2, 2)), dma((2, 2)),
            dma, dma, dma, dma, dma((4,)), dma,
        ],
        compiler_params=pltpu.CompilerParams(
            collective_id=0, has_side_effects=True, vmem_limit_bytes=60 * 2**20
        ),
        cost_estimate=pl.CostEstimate(flops=12 * 10**9, bytes_accessed=8 * 2**20, transcendentals=10**6),
    )(*args)


def body(
    homolog_embedding,
    alignment_mask,
    pairwise_features,
    residue_validity_mask,
    left_right_coefficients,
    outer_output_weight,
    triangle_input_weight,
    triangle_gate_weight,
    triangle_output_weight,
):
    edge_weights = jnp.transpose(triangle_input_weight, (0, 2, 1)).reshape(C_Z, C_Z)
    return call(
        homolog_embedding, alignment_mask, pairwise_features, left_right_coefficients.T,
        outer_output_weight, edge_weights, triangle_gate_weight.T, triangle_output_weight,
        residue_validity_mask, residue_validity_mask.reshape(4, 128),
    )


def solution(mesh):
    return jax.shard_map(
        body,
        mesh=mesh,
        in_specs=(
            P(("dapw", "dapn"), None, None),
            P(("dapw", "dapn"), None),
            P("dapn", "dapw", None),
            P(),
            P(),
            P(),
            P(None, None, "dapn"),
            P(None, "dapn"),
            P(),
        ),
        out_specs=P("dapn", "dapw", None),
        check_vma=False,
    )
```
